128 devices in a mesh: dp: 16 (over x_lo, z, core), tensor: 8 (over y, x_hi).
Axes of the slice: x: 4 (x_hi: 2, x_lo: 2; x = x_hi * 2 + x_lo), y: 4, z: 4, core: 2. Of those that a mesh axis runs over, the one named last changes fastest.
Arguments:
- queries: bfloat16 [49152, 1024], P('dp', 'tensor'), may hold values from -80 to 80
- keys: bfloat16 [49152, 128], P('dp'), may hold values from -6 to 6
- values: bfloat16 [49152, 128], P('dp'), may hold values from -6 to 6
- dout: bfloat16 [49152, 1024], P('dp', 'tensor'), may hold values from -6 to 6
- offsets: int32 [8], replicated, may hold values from 0 to 2047
- lengths: int32 [16], P('dp'), may hold values from 256 to 1024
Outputs:
- dq: bfloat16 [49152, 1024], P('dp', 'tensor')
- dk: bfloat16 [49152, 128], P('dp')
- dv: bfloat16 [49152, 128], P('dp')
The draws below stay inside these ranges and needn't reach their ends.
All inputs are finite; a program needn't handle non-finite values.
Results may differ from the reference program's by a relative error of at most 0.015.
Values may be sent and summed in bfloat16 or wider, within the bound.
A program may use at most 128 MiB of HBM per device.

```python
import jax
import jax.numpy as jnp

DH = 128
PH = 2048
R = 1024
HEADS = 8
PAIRS = 8
TOKENS = 49152
N_DP = 16


def shared_keys(key):
    first = jax.random.fold_in(key, 0)
    normal_keys = jnp.clip(jax.random.normal(first, (TOKENS, DH), jnp.float32), -6.0, 6.0)
    return normal_keys


def draw_keys(key, part):
    normal_keys = shared_keys(key)
    return normal_keys.astype(jnp.bfloat16)


def draw_queries(key, part):
    key = jax.random.fold_in(key, 7)
    first = jax.random.fold_in(key, 0)
    base = jnp.clip(jax.random.normal(first, (TOKENS, HEADS * DH), jnp.float32), -6.0, 6.0)
    return base.astype(jnp.bfloat16)


def touch_ends(result, own_key, least, largest):
    index_at = [jax.random.randint(jax.random.fold_in(own_key, axis), (), 0, length) for axis, length in enumerate(result.shape)]
    widest = result.shape.index(max(result.shape))
    beside = index_at[:widest] + [(index_at[widest] + 1) % result.shape[widest]] + index_at[widest + 1:]
    return result.at[tuple(index_at)].set(least).at[tuple(beside)].set(largest)


def block_levels(own_key, shape, pieces, smallest, largest):
    level, own = 1.0, jax.random.fold_in(own_key, 6)
    for axis_at, shards_of in pieces:
        steps = jnp.exp(jax.random.uniform(jax.random.fold_in(own, axis_at), (shards_of,), jnp.float32, smallest / len(pieces), largest / len(pieces)))
        level = level * jnp.repeat(steps, shape[axis_at] // shards_of).reshape([-1 if axis == axis_at else 1 for axis in range(len(shape))])
    return level


def normal_values(stream_key, dims, width, most, cuts=(), kind=jnp.bfloat16):
    factor_of = block_levels(stream_key, dims, cuts, -0.22, 0.18) if cuts else 1.0
    array = jax.random.normal(stream_key, dims, jnp.float32) * width * factor_of
    return jnp.minimum(jnp.maximum(array, -most), most).astype(kind)


def setup_inputs(seed: int = 0) -> dict:
    seeds = jax.random.split(jax.random.key(seed), 7)
    queries = draw_queries(jax.random.fold_in(seeds[6], 71), 0)
    keys = draw_keys(jax.random.fold_in(seeds[6], 71), 0)
    values = normal_values(seeds[2], (TOKENS, DH), 1.0, 6.0, ((0, 16),))
    dout = normal_values(seeds[3], (TOKENS, HEADS * DH), 1.0, 6.0, ((0, 16), (1, 8)))
    offsets = touch_ends(jax.random.randint(seeds[4], (PAIRS,), 0, PH), jax.random.fold_in(seeds[4], 1), 0, PH - 1).astype(jnp.int32)
    lengths = touch_ends(jax.random.randint(seeds[5], (N_DP,), R // 4, R + 1), jax.random.fold_in(seeds[5], 1), R // 4, R).astype(jnp.int32)
    return dict(queries=queries, keys=keys, values=values, dout=dout, offsets=offsets, lengths=lengths)


def head_terms(query, grad_out, positions, key_all, value_all, key_pos, offset):
    scale = 1.0 / (query.shape[1] ** 0.5)
    query32 = query.astype(jnp.float32)
    grad32 = grad_out.astype(jnp.float32)
    key32 = key_all.astype(jnp.float32)
    value32 = value_all.astype(jnp.float32)
    scores = jnp.dot(query32, key32.T) * scale
    allowed = (key_pos[None, :] <= positions[:, None]) & ((key_pos[None, :] >= offset) | (key_pos[None, :] == positions[:, None]))
    scores = jnp.where(allowed, scores, -jnp.inf)
    top = jnp.max(scores, axis=1, keepdims=True)
    expo = jnp.exp(scores - top)
    probs = expo / jnp.sum(expo, axis=1, keepdims=True)
    probs_b = probs.astype(jnp.bfloat16).astype(jnp.float32)
    output = jnp.dot(probs_b, value32)
    delta = jnp.sum(grad32 * output, axis=1)
    dprobs = jnp.dot(grad32, value32.T)
    dscores = (probs * (dprobs - delta[:, None]) * scale).astype(jnp.bfloat16).astype(jnp.float32)
    grad_q = jnp.dot(dscores, key32)
    grad_k = jnp.dot(dscores.T, query32)
    grad_v = jnp.dot(probs_b.T, grad32)
    return grad_q, grad_k, grad_v


def member_terms(queries, dout, key_all, value_all, side, offset, length):
    head_dim = key_all.shape[1]
    heads = queries.shape[1] // head_dim
    positions = jnp.concatenate([side * PH + jnp.arange(PH, dtype=jnp.int32), 2 * PH + jnp.arange(R, dtype=jnp.int32)])
    valid = jnp.concatenate([jnp.ones((PH,), jnp.bool_), jnp.arange(R, dtype=jnp.int32) < length])
    masked = jnp.where(valid[:, None], dout, jnp.zeros_like(dout))
    key_pos = jnp.arange(2 * PH + R, dtype=jnp.int32)
    grad_qs = []
    grad_k = jnp.zeros((2 * PH + R, head_dim), jnp.float32)
    grad_v = jnp.zeros((2 * PH + R, head_dim), jnp.float32)
    for head in range(heads):
        cols = slice(head * head_dim, (head + 1) * head_dim)
        gq, gk, gv = head_terms(queries[:, cols], masked[:, cols], positions, key_all, value_all, key_pos, offset)
        grad_qs.append(gq.astype(jnp.bfloat16))
        grad_k = grad_k + gk
        grad_v = grad_v + gv
    return jnp.concatenate(grad_qs, axis=1), grad_k, grad_v


def reference(queries, keys, values, dout, offsets, lengths):
    rows = PH + R
    pairs = N_DP // 2
    dq_parts = [None] * N_DP
    dk_parts = [None] * N_DP
    dv_parts = [None] * N_DP
    for pair in range(pairs):
        chosen, rejected = pair, pair + pairs
        sl_c = slice(chosen * rows, (chosen + 1) * rows)
        sl_r = slice(rejected * rows, (rejected + 1) * rows)
        prompt_k = jnp.concatenate([keys[sl_c][:PH], keys[sl_r][:PH]])
        prompt_v = jnp.concatenate([values[sl_c][:PH], values[sl_r][:PH]])
        results = []
        for side, sl, member in ((0, sl_c, chosen), (1, sl_r, rejected)):
            key_all = jnp.concatenate([prompt_k, keys[sl][PH:]])
            value_all = jnp.concatenate([prompt_v, values[sl][PH:]])
            results.append(member_terms(queries[sl], dout[sl], key_all, value_all, side, offsets[pair], lengths[member]))
        (gq_c, gk_c, gv_c), (gq_r, gk_r, gv_r) = results
        prompt_gk = gk_c[:2 * PH] + gk_r[:2 * PH]
        prompt_gv = gv_c[:2 * PH] + gv_r[:2 * PH]
        dq_parts[chosen] = gq_c
        dq_parts[rejected] = gq_r
        dk_parts[chosen] = jnp.concatenate([prompt_gk[:PH], gk_c[2 * PH:]]).astype(jnp.bfloat16)
        dk_parts[rejected] = jnp.concatenate([prompt_gk[PH:], gk_r[2 * PH:]]).astype(jnp.bfloat16)
        dv_parts[chosen] = jnp.concatenate([prompt_gv[:PH], gv_c[2 * PH:]]).astype(jnp.bfloat16)
        dv_parts[rejected] = jnp.concatenate([prompt_gv[PH:], gv_r[2 * PH:]]).astype(jnp.bfloat16)
    return jnp.concatenate(dq_parts), jnp.concatenate(dk_parts), jnp.concatenate(dv_parts)
```

```python
import functools

import jax
import jax.numpy as jnp
from jax import lax
from jax.experimental import pallas as pl
from jax.experimental.pallas import tpu as pltpu
from jax.sharding import PartitionSpec as P

MESH = pl.DeviceIdType.MESH
f32 = jnp.float32
bf = jnp.bfloat16

PH = 2048
R = 1024
DH = 128
KEYS = 2 * PH + R
BQ, BK = 256, 512
RG = 64
NT = 8
SLP = PH // NT
SLR = R // NT
NEG = -1e30
SCALE = 1.0 / DH**0.5
CC = SCALE * 1.4426950408889634


def dot_nt(a, b):
    return lax.dot_general(a, b, (((1,), (1,)), ((), ())), preferred_element_type=f32)


def dot_nn(a, b):
    return jnp.dot(a, b, preferred_element_type=f32)


def kernel(
    offs, lens, q, kin, vin, do, dq, dk, dv,
    k, v, dkT, dvT, S0, S1, DP0, DP1, E, P0, P1, D0, D1, mx, mb, la, ta, dqa, dom, qT, dT, bias,
    sendP, sendR, recvP, recvR,
    kv_s, kv_r, p_s, p_r, r_s, r_r, g_s, g_r,
):
    d = lax.axis_index("dp")
    t = lax.axis_index("tensor")
    half = lax.axis_size("dp") // 2
    side = lax.div(d, half)
    pair = lax.rem(d, half)
    offset = offs[pair]
    length = lens[0]

    def peer(b, a):
        return (lax.rem(side + b, 2) * half + pair, lax.rem(t + a, NT))

    barrier = pltpu.get_barrier_semaphore()
    for i in range(1, 2 * NT):
        pl.semaphore_signal(barrier, inc=1, device_id=peer(i // NT, i % NT), device_id_type=MESH)
    pl.semaphore_wait(barrier, 2 * NT - 1)

    flip = t + 1 - 2 * lax.rem(t, 2)
    hp = PH // 2
    kv = []
    for h in range(2):
        dst = (lax.rem(side + 1, 2) * half + pair, t if h == 0 else flip)
        for i, (src, to) in enumerate(((kin, k), (vin, v))):
            rows = pl.ds(pl.multiple_of(side * PH + h * hp, hp), hp)
            c = pltpu.make_async_remote_copy(
                src_ref=src.at[pl.ds(h * hp, hp)], dst_ref=to.at[rows],
                send_sem=kv_s.at[2 * h + i], recv_sem=kv_r.at[2 * h + i],
                device_id=dst, device_id_type=MESH,
            )
            c.start()
            kv.append(c)

    own = pl.ds(pl.multiple_of(side * PH, PH), PH)
    k[own, :] = kin[:PH, :]
    v[own, :] = vin[:PH, :]
    k[2 * PH :, :] = kin[PH:, :]
    v[2 * PH :, :] = vin[PH:, :]
    dom[:PH, :] = do[:PH, :]
    rr = lax.broadcasted_iota(jnp.int32, (R, DH), 0)
    dom[PH:, :] = jnp.where(rr < length, do[PH:, :], jnp.zeros((R, DH), bf))
    kp = lax.broadcasted_iota(jnp.int32, (8, KEYS), 1)
    bias[...] = jnp.where(kp >= offset, 0.0, NEG).astype(f32)
    dkT[...] = jnp.zeros_like(dkT)
    dvT[...] = jnp.zeros_like(dvT)
    for c in kv:
        c.wait_recv()

    NR, NP = R // BQ, PH // BQ
    NB = NR + NP
    T = BK // 128
    SS, DPS, PS, DS = (S0, S1), (DP0, DP1), (P0, P1), (D0, D1)

    def info(j):
        row0 = jnp.where(j < NR, PH + j * BQ, (NP - 1 - (j - NR)) * BQ)
        pos0 = jnp.where(j < NR, 2 * PH + j * BQ, side * PH + row0)
        return pl.multiple_of(row0, BQ), pos0, lax.div(pos0 + BQ - 1, BK) + 1

    def ks(c):
        return pl.ds(pl.multiple_of(c * BK, BK), BK)

    def kt(c, i):
        return pl.ds(pl.multiple_of(c * BK + i * 128, 128), 128)

    def scores(slot, row0, pos0, c, masked):
        S, DP = SS[slot], DPS[slot]
        s = dot_nt(q[pl.ds(row0, BQ), :], k[ks(c), :])
        if masked:
            cols = lax.broadcasted_iota(jnp.int32, (RG, 128), 1)
        for r in range(0, BQ, RG):
            m = mx[r : r + RG, :]
            for i in range(T):
                st = s[r : r + RG, i * 128 : (i + 1) * 128]
                if masked:
                    rows = lax.broadcasted_iota(jnp.int32, (RG, 128), 0) + (pos0 - c * BK + r)
                    ct = cols + i * 128
                    ok = (ct < rows) & (ct + c * BK >= offset) | (ct == rows)
                    st = jnp.where(ok, st, NEG)
                else:
                    st = st + bias[0:1, kt(c, i)]
                S[r : r + RG, kt(c, i)] = st
                m = jnp.maximum(m, st)
            mx[r : r + RG, :] = m
        DP[:, ks(c)] = dot_nt(dom[pl.ds(row0, BQ), :], v[ks(c), :])

    def row_max():
        mb[...] = jnp.broadcast_to(jnp.max(mx[...], axis=1, keepdims=True) * CC, (BQ, 128))
        mx[...] = jnp.full((BQ, 128), NEG, f32)

    def expo(slot, c):
        S, DP = SS[slot], DPS[slot]
        for r in range(0, BQ, RG):
            l, tt, m = la[r : r + RG, :], ta[r : r + RG, :], mb[r : r + RG, :]
            for i in range(T):
                e = jnp.exp2(S[r : r + RG, kt(c, i)] * CC - m)
                l = l + e
                tt = tt + e * DP[r : r + RG, kt(c, i)]
                E[r : r + RG, kt(c, i)] = e
            la[r : r + RG, :] = l
            ta[r : r + RG, :] = tt

    def grads_in(slot, h, c2):
        DP, Pb, Db = DPS[slot], PS[h], DS[h]
        for r in range(0, BQ, RG):
            rl, dl = la[r : r + RG, :], ta[r : r + RG, :]
            for i in range(2):
                sl = pl.ds(pl.multiple_of(c2 * 256 + i * 128, 128), 128)
                p = E[r : r + RG, sl] * rl
                x = p * (DP[r : r + RG, sl] - dl)
                Pb[r : r + RG, i * 128 : (i + 1) * 128] = p.astype(bf)
                Db[r : r + RG, i * 128 : (i + 1) * 128] = x.astype(bf)

    def grads_out(h, c2):
        Pb, Db = PS[h], DS[h]
        sl = pl.ds(pl.multiple_of(c2 * 256, 256), 256)
        dvT[:, sl] += dot_nn(dT[...], Pb[...])
        dkT[:, sl] += dot_nn(qT[...], Db[...])
        dqa[...] += dot_nn(Db[...], k[sl, :])

    def loop(lo, hi, f):
        def body(c, _):
            f(c)
            return 0

        lax.fori_loop(lo, hi, body, 0)

    def prompt_copy(b, a):
        ts = lax.rem(t + a, NT)
        ss = lax.rem(side + b, 2)
        return pltpu.make_async_remote_copy(
            src_ref=sendP.at[ss * NT + ts], dst_ref=recvP.at[b * NT + a],
            send_sem=p_s.at[b * NT + a], recv_sem=p_r.at[b * NT + a],
            device_id=peer(b, a), device_id_type=MESH,
        )

    def resp_copy(a):
        ts = lax.rem(t + a, NT)
        return pltpu.make_async_remote_copy(
            src_ref=sendR.at[ts], dst_ref=recvR.at[a],
            send_sem=r_s.at[a], recv_sem=r_r.at[a],
            device_id=peer(0, a), device_id_type=MESH,
        )

    def pack_prompt(i):
        sl = pl.ds(pl.multiple_of(i * SLP, SLP), SLP)
        sendP[i, :DH, :] = (dkT[:, sl] * SCALE).astype(bf)
        sendP[i, DH:, :] = dvT[:, sl].astype(bf)

    def send_other():
        loop(0, NT, lambda i: pack_prompt(lax.rem(side + 1, 2) * NT + i))
        for a in range(NT):
            prompt_copy(1, a).start()

    def send_resp():
        for i in range(NT):
            sl = slice(2 * PH + i * SLR, 2 * PH + (i + 1) * SLR)
            sendR[i, :DH, :] = (dkT[:, sl] * SCALE).astype(bf)
            sendR[i, DH:, :] = dvT[:, sl].astype(bf)
        for a in range(1, NT):
            resp_copy(a).start()

    mx[...] = jnp.full((BQ, 128), NEG, f32)
    row0, pos0, n0 = info(jnp.int32(0))
    loop(0, n0 - 1, lambda c: scores(0, row0, pos0, c, False))
    scores(0, row0, pos0, n0 - 1, True)
    row_max()

    def block(j, slot):
        nxt = 1 - slot
        row0, _, n = info(j)
        row1, pos1, n1 = info(j + 1)
        la[...] = jnp.zeros((BQ, 128), f32)
        ta[...] = jnp.zeros((BQ, 128), f32)
        last = j == NB - 1
        na = jnp.where(last, 0, n1 - 1)
        m = jnp.minimum(na, n)

        def both(c):
            expo(slot, c)
            scores(nxt, row1, pos1, c, False)

        loop(0, m, both)
        loop(m, na, lambda c: scores(nxt, row1, pos1, c, False))
        loop(m, n, lambda c: expo(slot, c))
        rl = 1.0 / jnp.sum(la[...], axis=1, keepdims=True)
        dl = jnp.sum(ta[...], axis=1, keepdims=True) * rl
        la[...] = jnp.broadcast_to(rl, (BQ, 128))
        ta[...] = jnp.broadcast_to(dl, (BQ, 128))

        @pl.when(jnp.logical_not(last))
        def _():
            scores(nxt, row1, pos1, n1 - 1, True)
            row_max()

        qT[...] = q[pl.ds(row0, BQ), :].T
        dT[...] = dom[pl.ds(row0, BQ), :].T
        dqa[...] = jnp.zeros((BQ, DH), f32)
        grads_in(slot, 0, 0)

        def pipe(c):
            grads_out(0, 2 * c)
            grads_in(slot, 1, 2 * c + 1)
            grads_out(1, 2 * c + 1)
            grads_in(slot, 0, 2 * c + 2)

        loop(0, n, pipe)
        dq[pl.ds(row0, BQ), :] = (dqa[...] * SCALE).astype(bf)

        @pl.when(j == NR - 1)
        def _():
            send_resp()

            @pl.when(side == 0)
            def _():
                send_other()

        @pl.when(j >= NR)
        def _():
            b = NP - 1 - (j - NR)
            pack_prompt(side * NT + b)
            for a in range(1, NT):

                @pl.when(lax.rem(t + a, NT) == b)
                def _():
                    prompt_copy(0, a).start()

    def two(i):
        block(2 * i, 0)
        block(2 * i + 1, 1)

    loop(0, NB // 2, two)

    @pl.when(side == 1)
    def _():
        send_other()

    def gather(rows, i, a):
        return [
            pltpu.make_async_remote_copy(
                src_ref=o.at[rows], dst_ref=o.at[rows],
                send_sem=g_s.at[2 * i + w, a], recv_sem=g_r.at[2 * i + w, a],
                device_id=peer(0, a), device_id_type=MESH,
            )
            for w, o in enumerate((dk, dv))
        ]

    rrows = pl.ds(pl.multiple_of(PH + t * SLR, SLR), SLR)
    prows = pl.ds(pl.multiple_of(t * SLP, SLP), SLP)
    total = sendR[t].astype(f32)
    for a in range(1, NT):
        resp_copy(a).wait_recv()
        total = total + recvR[a].astype(f32)
    dk[rrows, :] = total[:DH, :].T.astype(bf)
    dv[rrows, :] = total[DH:, :].T.astype(bf)
    for a in range(1, NT):
        for c in gather(rrows, 0, a):
            c.start()
    total = sendP[side * NT + t].astype(f32)
    for i in range(1, 2 * NT):
        prompt_copy(i // NT, i % NT).wait_recv()
        total = total + recvP[i].astype(f32)
    dk[prows, :] = total[:DH, :].T.astype(bf)
    dv[prows, :] = total[DH:, :].T.astype(bf)
    for a in range(1, NT):
        for c in gather(prows, 1, a):
            c.start()
    for c in kv:
        c.wait_send()
    for i in range(1, 2 * NT):
        prompt_copy(i // NT, i % NT).wait_send()
    for a in range(1, NT):
        resp_copy(a).wait_send()
        for c in gather(rrows, 0, a) + gather(prows, 1, a):
            c.wait()


def per_device(queries, keys, values, dout, offsets, lengths):
    V = pl.BlockSpec(memory_space=pltpu.VMEM)
    SM = pl.BlockSpec(memory_space=pltpu.SMEM)
    D = pltpu.SemaphoreType.DMA
    rows = PH + R
    big = pltpu.VMEM((BQ, KEYS + 256), f32)
    stat = pltpu.VMEM((BQ, 128), f32)
    return tuple(
        pl.pallas_call(
            kernel,
            out_shape=[jax.ShapeDtypeStruct((rows, DH), bf)] * 3,
            in_specs=[SM, SM, V, V, V, V],
            out_specs=[V, V, V],
            scratch_shapes=[
                pltpu.VMEM((KEYS, DH), bf), pltpu.VMEM((KEYS, DH), bf),
                pltpu.VMEM((DH, KEYS), f32), pltpu.VMEM((DH, KEYS), f32),
                big, big, big, big, big,
                *[pltpu.VMEM((BQ, 256), bf)] * 4,
                stat, stat, stat, stat,
                pltpu.VMEM((BQ, DH), f32), pltpu.VMEM((rows, DH), bf),
                pltpu.VMEM((DH, BQ), bf), pltpu.VMEM((DH, BQ), bf),
                pltpu.VMEM((8, KEYS), f32),
                pltpu.VMEM((2 * NT, 2 * DH, SLP), bf), pltpu.VMEM((NT, 2 * DH, SLR), bf),
                pltpu.VMEM((2 * NT, 2 * DH, SLP), bf), pltpu.VMEM((NT, 2 * DH, SLR), bf),
                D((4,)), D((4,)), D((2 * NT,)), D((2 * NT,)), D((NT,)), D((NT,)),
                D((4, NT)), D((4, NT)),
            ],
            compiler_params=pltpu.CompilerParams(
                collective_id=0, has_side_effects=True, vmem_limit_bytes=60 * 2**20
            ),
        )(offsets, lengths, queries, keys, values, dout)
    )


def solution(mesh):
    return jax.shard_map(
        per_device,
        mesh=mesh,
        in_specs=(P("dp", "tensor"), P("dp", None), P("dp", None), P("dp", "tensor"), P(), P("dp")),
        out_specs=(P("dp", "tensor"), P("dp", None), P("dp", None)),
        check_vma=False,
    )
```

```python
import functools

import jax
import jax.numpy as jnp
from jax import lax
from jax.experimental import pallas as pl
from jax.experimental.pallas import tpu as pltpu
from jax.sharding import PartitionSpec as P

MESH = pl.DeviceIdType.MESH
f32 = jnp.float32
bf = jnp.bfloat16

PH = 2048
R = 1024
DH = 128
KEYS = 2 * PH + R
BQ, BK = 256, 512
RG = 16
T = BK // 128
NT = 8
SLP = PH // NT
SLR = R // NT
NEG = -1e30
SCALE = 1.0 / DH**0.5
CC = SCALE * 1.4426950408889634


def dot_nt(a, b):
    return lax.dot_general(a, b, (((1,), (1,)), ((), ())), preferred_element_type=f32)


def dot_nn(a, b):
    return jnp.dot(a, b, preferred_element_type=f32)


def kernel(
    offs, lens, q, kin, vin, do, dq, dk, dv,
    k, v, dkT, dvT, S, E, DP0, DP1, mx, mb, la, ta, rl, dl, dqa, dom, qT, dT, bias,
    sendP, sendR, recvP, recvR,
    kv_s, kv_r, p_s, p_r, r_s, r_r, g_s, g_r,
):
    d = lax.axis_index("dp")
    t = lax.axis_index("tensor")
    half = lax.axis_size("dp") // 2
    side = lax.div(d, half)
    pair = lax.rem(d, half)
    offset = offs[pair]
    length = lens[0]

    def peer(b, a):
        return (lax.rem(side + b, 2) * half + pair, lax.rem(t + a, NT))

    barrier = pltpu.get_barrier_semaphore()
    for i in range(1, 2 * NT):
        pl.semaphore_signal(barrier, inc=1, device_id=peer(i // NT, i % NT), device_id_type=MESH)
    pl.semaphore_wait(barrier, 2 * NT - 1)

    flip = t + 1 - 2 * lax.rem(t, 2)
    hp = PH // 2
    kv = []
    for h in range(2):
        dst = (lax.rem(side + 1, 2) * half + pair, t if h == 0 else flip)
        for i, (src, to) in enumerate(((kin, k), (vin, v))):
            rows = pl.ds(pl.multiple_of(side * PH + h * hp, hp), hp)
            c = pltpu.make_async_remote_copy(
                src_ref=src.at[pl.ds(h * hp, hp)], dst_ref=to.at[rows],
                send_sem=kv_s.at[2 * h + i], recv_sem=kv_r.at[2 * h + i],
                device_id=dst, device_id_type=MESH,
            )
            c.start()
            kv.append(c)

    own = pl.ds(pl.multiple_of(side * PH, PH), PH)
    k[own, :] = kin[:PH, :]
    v[own, :] = vin[:PH, :]
    k[2 * PH :, :] = kin[PH:, :]
    v[2 * PH :, :] = vin[PH:, :]
    dom[:PH, :] = do[:PH, :]
    rr = lax.broadcasted_iota(jnp.int32, (R, DH), 0)
    dom[PH:, :] = jnp.where(rr < length, do[PH:, :], jnp.zeros((R, DH), bf))
    kp = lax.broadcasted_iota(jnp.int32, (8, KEYS), 1)
    bias[...] = jnp.where(kp >= offset, 0.0, NEG).astype(f32)
    dkT[...] = jnp.zeros_like(dkT)
    dvT[...] = jnp.zeros_like(dvT)
    for c in kv:
        c.wait_recv()

    NR, NP = R // BQ, PH // BQ
    NB = NR + NP
    DPS = (DP0, DP1)

    def info(j):
        row0 = jnp.where(j < NR, PH + (NR - 1 - j) * BQ, (NB - 1 - j) * BQ)
        pos0 = jnp.where(j < NR, PH + row0, side * PH + row0)
        n = jnp.where(j < NB, lax.div(pos0 + BQ - 1, BK) + 1, 0)
        return pl.multiple_of(jnp.maximum(row0, 0), BQ), pos0, n

    def ks(c):
        return pl.ds(pl.multiple_of(c * BK, BK), BK)

    def scores(slot, row0, pos0, c, masked):
        DP = DPS[slot]
        s = dot_nt(q[pl.ds(row0, BQ), :], k[ks(c), :])
        dp = dot_nt(dom[pl.ds(row0, BQ), :], v[ks(c), :])
        if masked:
            cols = lax.broadcasted_iota(jnp.int32, (RG, 128), 1)
        for r in range(0, BQ, RG):
            m = mx[r : r + RG, :]
            for i in range(T):
                st = s[r : r + RG, i * 128 : (i + 1) * 128]
                if masked:
                    rows = lax.broadcasted_iota(jnp.int32, (RG, 128), 0) + (pos0 - c * BK + r)
                    ct = cols + i * 128
                    ok = (ct < rows) & (ct + c * BK >= offset) | (ct == rows)
                    st = jnp.where(ok, st, NEG)
                else:
                    st = st + bias[0:1, pl.ds(pl.multiple_of(c * BK + i * 128, 128), 128)]
                S[c * T + i, r : r + RG, :] = st
                m = jnp.maximum(m, st)
                DP[c * T + i, r : r + RG, :] = dp[r : r + RG, i * 128 : (i + 1) * 128]
            mx[r : r + RG, :] = m

    def expo(slot, c):
        DP = DPS[slot]
        for r in range(0, BQ, RG):
            l, tt, m = la[r : r + RG, :], ta[r : r + RG, :], mb[r : r + RG, :]
            for i in range(T):
                e = jnp.exp2(S[c * T + i, r : r + RG, :] * CC - m)
                l = l + e
                tt = tt + e * DP[c * T + i, r : r + RG, :]
                E[c * T + i, r : r + RG, :] = e
            la[r : r + RG, :] = l
            ta[r : r + RG, :] = tt

    def grads_in(slot, c):
        DP = DPS[slot]
        ps, xs = [], []
        for r in range(0, BQ, RG):
            rv, dd = rl[r : r + RG, :], dl[r : r + RG, :]
            pr, xr = [], []
            for i in range(T):
                p = E[c * T + i, r : r + RG, :] * rv
                x = p * (DP[c * T + i, r : r + RG, :] - dd)
                pr.append(p.astype(bf))
                xr.append(x.astype(bf))
            ps.append(jnp.concatenate(pr, 1))
            xs.append(jnp.concatenate(xr, 1))
        return jnp.concatenate(ps, 0), jnp.concatenate(xs, 0)

    def grads_out(c, p, x):
        gv = dot_nn(dT[...], p)
        gk = dot_nn(qT[...], x)
        for i in range(T):
            dvT[c * T + i] += gv[:, i * 128 : (i + 1) * 128]
            dkT[c * T + i] += gk[:, i * 128 : (i + 1) * 128]
        dqa[...] += dot_nn(x, k[ks(c), :])

    def row_max():
        mb[...] = jnp.broadcast_to(jnp.max(mx[...], axis=1, keepdims=True) * CC, (BQ, 128))
        mx[...] = jnp.full((BQ, 128), NEG, f32)

    def row_sums():
        inv = 1.0 / jnp.sum(la[...], axis=1, keepdims=True)
        rl[...] = jnp.broadcast_to(inv, (BQ, 128))
        dl[...] = jnp.broadcast_to(jnp.sum(ta[...], axis=1, keepdims=True) * inv, (BQ, 128))
        la[...] = jnp.zeros((BQ, 128), f32)
        ta[...] = jnp.zeros((BQ, 128), f32)

    def turn(row):
        qT[...] = q[pl.ds(row, BQ), :].T
        dT[...] = dom[pl.ds(row, BQ), :].T
        dqa[...] = jnp.zeros((BQ, DH), f32)

    def loop(lo, hi, f):
        def body(c, _):
            f(c)
            return 0

        lax.fori_loop(lo, hi, body, 0)

    def prompt_copy(b, a):
        ts = lax.rem(t + a, NT)
        ss = lax.rem(side + b, 2)
        return pltpu.make_async_remote_copy(
            src_ref=sendP.at[ss * NT + ts], dst_ref=recvP.at[b * NT + a],
            send_sem=p_s.at[b * NT + a], recv_sem=p_r.at[b * NT + a],
            device_id=peer(b, a), device_id_type=MESH,
        )

    def resp_copy(a):
        ts = lax.rem(t + a, NT)
        return pltpu.make_async_remote_copy(
            src_ref=sendR.at[ts], dst_ref=recvR.at[a],
            send_sem=r_s.at[a], recv_sem=r_r.at[a],
            device_id=peer(0, a), device_id_type=MESH,
        )

    def pack(to, at, i0, tiles):
        for i in range(tiles):
            to[at, :DH, i * 128 : (i + 1) * 128] = (dkT[i0 + i] * SCALE).astype(bf)
            to[at, DH:, i * 128 : (i + 1) * 128] = dvT[i0 + i].astype(bf)

    def pack_prompt(i):
        pack(sendP, i, i * (SLP // 128), SLP // 128)

    def send_other():
        loop(0, NT, lambda i: pack_prompt(lax.rem(side + 1, 2) * NT + i))
        for a in range(NT):
            prompt_copy(1, a).start()

    def send_resp():
        for i in range(NT):
            pack(sendR, i, (2 * PH + i * SLR) // 128, SLR // 128)
        for a in range(1, NT):
            resp_copy(a).start()

    mx[...] = jnp.full((BQ, 128), NEG, f32)
    la[...] = jnp.zeros((BQ, 128), f32)
    ta[...] = jnp.zeros((BQ, 128), f32)
    ra, pa, na = info(jnp.int32(0))
    rb, pb, nb = info(jnp.int32(1))
    loop(0, na - 1, lambda c: scores(0, ra, pa, c, False))
    scores(0, ra, pa, na - 1, True)
    row_max()

    def first(c, masked=False):
        expo(0, c)
        scores(1, rb, pb, c, masked)

    loop(0, nb - 1, first)
    first(nb - 1, True)
    loop(nb, na, lambda c: expo(0, c))
    row_sums()
    row_max()
    turn(ra)

    def block(j, slot):
        r0, _, n0 = info(j)
        r1, _, n1 = info(j + 1)
        r2, p2, n2 = info(j + 2)

        def three(c, masked=False):
            p, x = grads_in(slot, c)
            expo(1 - slot, c)
            scores(slot, r2, p2, c, masked)
            grads_out(c, p, x)

        def two_of(c):
            p, x = grads_in(slot, c)
            expo(1 - slot, c)
            grads_out(c, p, x)

        def one_of(c):
            grads_out(c, *grads_in(slot, c))

        loop(0, n2 - 1, three)

        @pl.when(n2 > 0)
        def _():
            three(n2 - 1, True)

        loop(n2, n1, two_of)
        loop(n1, n0, one_of)
        dq[pl.ds(r0, BQ), :] = (dqa[...] * SCALE).astype(bf)

        @pl.when(n1 > 0)
        def _():
            row_sums()
            row_max()
            turn(r1)

        @pl.when(j == NR - 1)
        def _():
            send_resp()

            @pl.when(side == 0)
            def _():
                send_other()

        @pl.when(j >= NR)
        def _():
            b = NP - 1 - (j - NR)
            pack_prompt(side * NT + b)
            for a in range(1, NT):

                @pl.when(lax.rem(t + a, NT) == b)
                def _():
                    prompt_copy(0, a).start()

    def two(i):
        block(2 * i, 0)
        block(2 * i + 1, 1)

    loop(0, NB // 2, two)

    @pl.when(side == 1)
    def _():
        send_other()

    def gather(rows, i, a):
        return [
            pltpu.make_async_remote_copy(
                src_ref=o.at[rows], dst_ref=o.at[rows],
                send_sem=g_s.at[2 * i + w, a], recv_sem=g_r.at[2 * i + w, a],
                device_id=peer(0, a), device_id_type=MESH,
            )
            for w, o in enumerate((dk, dv))
        ]

    rrows = pl.ds(pl.multiple_of(PH + t * SLR, SLR), SLR)
    prows = pl.ds(pl.multiple_of(t * SLP, SLP), SLP)
    total = sendR[t].astype(f32)
    for a in range(1, NT):
        resp_copy(a).wait_recv()
        total = total + recvR[a].astype(f32)
    dk[rrows, :] = total[:DH, :].T.astype(bf)
    dv[rrows, :] = total[DH:, :].T.astype(bf)
    for a in range(1, NT):
        for c in gather(rrows, 0, a):
            c.start()
    total = sendP[side * NT + t].astype(f32)
    for i in range(1, 2 * NT):
        prompt_copy(i // NT, i % NT).wait_recv()
        total = total + recvP[i].astype(f32)
    dk[prows, :] = total[:DH, :].T.astype(bf)
    dv[prows, :] = total[DH:, :].T.astype(bf)
    for a in range(1, NT):
        for c in gather(prows, 1, a):
            c.start()
    for c in kv:
        c.wait_send()
    for i in range(1, 2 * NT):
        prompt_copy(i // NT, i % NT).wait_send()
    for a in range(1, NT):
        resp_copy(a).wait_send()
        for c in gather(rrows, 0, a) + gather(prows, 1, a):
            c.wait()


def per_device(queries, keys, values, dout, offsets, lengths):
    V = pl.BlockSpec(memory_space=pltpu.VMEM)
    SM = pl.BlockSpec(memory_space=pltpu.SMEM)
    D = pltpu.SemaphoreType.DMA
    rows = PH + R
    big = pltpu.VMEM((KEYS // 128, BQ, 128), f32)
    acc = pltpu.VMEM((KEYS // 128, DH, 128), f32)
    stat = pltpu.VMEM((BQ, 128), f32)
    return tuple(
        pl.pallas_call(
            kernel,
            out_shape=[jax.ShapeDtypeStruct((rows, DH), bf)] * 3,
            in_specs=[SM, SM, V, V, V, V],
            out_specs=[V, V, V],
            scratch_shapes=[
                pltpu.VMEM((KEYS, DH), bf), pltpu.VMEM((KEYS, DH), bf),
                acc, acc, big, big, big, big,
                stat, stat, stat, stat, stat, stat,
                pltpu.VMEM((BQ, DH), f32), pltpu.VMEM((rows, DH), bf),
                pltpu.VMEM((DH, BQ), bf), pltpu.VMEM((DH, BQ), bf),
                pltpu.VMEM((8, KEYS), f32),
                pltpu.VMEM((2 * NT, 2 * DH, SLP), bf), pltpu.VMEM((NT, 2 * DH, SLR), bf),
                pltpu.VMEM((2 * NT, 2 * DH, SLP), bf), pltpu.VMEM((NT, 2 * DH, SLR), bf),
                D((4,)), D((4,)), D((2 * NT,)), D((2 * NT,)), D((NT,)), D((NT,)),
                D((4, NT)), D((4, NT)),
            ],
            compiler_params=pltpu.CompilerParams(
                collective_id=0, has_side_effects=True, vmem_limit_bytes=60 * 2**20
            ),
        )(offsets, lengths, queries, keys, values, dout)
    )


def solution(mesh):
    return jax.shard_map(
        per_device,
        mesh=mesh,
        in_specs=(P("dp", "tensor"), P("dp", None), P("dp", None), P("dp", "tensor"), P(), P("dp")),
        out_specs=(P("dp", "tensor"), P("dp", None), P("dp", None)),
        check_vma=False,
    )
```

```python
import functools

import jax
import jax.numpy as jnp
from jax import lax
from jax.experimental import pallas as pl
from jax.experimental.pallas import tpu as pltpu
from jax.sharding import PartitionSpec as P

MESH = pl.DeviceIdType.MESH
f32 = jnp.float32
bf = jnp.bfloat16

PH = 2048
R = 1024
DH = 128
KEYS = 2 * PH + R
BQ, BK = 256, 512
RG = 16
T = BK // 128
NT = 8
FT = 2 * DH // NT
HP = PH // 2
XR = 512
ROWS = PH + R
NEG = -1e30
SCALE = 1.0 / DH**0.5
CC = SCALE * 1.4426950408889634


def dot_nt(a, b):
    return lax.dot_general(a, b, (((1,), (1,)), ((), ())), preferred_element_type=f32)


def dot_nn(a, b):
    return jnp.dot(a, b, preferred_element_type=f32)


def kernel(
    offs, lens, q, kin, vin, do, dq, dk, dv,
    k, v, dkT, dvT, S, E, DP0, DP1, mx, mb, la, ta, rl, dl, dqa, dom, qT, dT, bias,
    qa, dqx, sb, rb, rr, ga,
    kv_s, kv_r, p_s, p_r, r_s, r_r, g_s, g_r, x_s, x_r,
):
    d = lax.axis_index("dp")
    t = lax.axis_index("tensor")
    half = lax.axis_size("dp") // 2
    side = lax.div(d, half)
    pair = lax.rem(d, half)
    offset = offs[pair]
    length = lens[0]

    def peer(b, a):
        return (lax.rem(side + b, 2) * half + pair, lax.rem(t + a, NT))

    barrier = pltpu.get_barrier_semaphore()
    for i in range(1, 2 * NT):
        pl.semaphore_signal(barrier, inc=1, device_id=peer(i // NT, i % NT), device_id_type=MESH)
    pl.semaphore_wait(barrier, 2 * NT - 1)

    flip = t + 1 - 2 * lax.rem(t, 2)
    kv = []
    for h in range(2):
        dst = (lax.rem(side + 1, 2) * half + pair, t if h == 0 else flip)
        for i, (src, to) in enumerate(((kin, k), (vin, v))):
            rows = pl.ds(pl.multiple_of(side * PH + h * HP, HP), HP)
            c = pltpu.make_async_remote_copy(
                src_ref=src.at[pl.ds(h * HP, HP)], dst_ref=to.at[rows],
                send_sem=kv_s.at[2 * h + i], recv_sem=kv_r.at[2 * h + i],
                device_id=dst, device_id_type=MESH,
            )
            c.start()
            kv.append(c)

    over = [
        pltpu.make_async_remote_copy(
            src_ref=src.at[pl.ds(PH - XR, XR)], dst_ref=to.at[pl.ds(ROWS, XR)],
            send_sem=x_s.at[i], recv_sem=x_r.at[i], device_id=peer(1, 0), device_id_type=MESH,
        )
        for i, (src, to) in enumerate(((q, qa), (do, dom)))
    ]
    back = pltpu.make_async_remote_copy(
        src_ref=dqx, dst_ref=dq.at[pl.ds(PH - XR, XR)],
        send_sem=x_s.at[2], recv_sem=x_r.at[2], device_id=peer(1, 0), device_id_type=MESH,
    )

    @pl.when(side == 1)
    def _():
        for c in over:
            c.start()

    own = pl.ds(pl.multiple_of(side * PH, PH), PH)
    qa[:ROWS, :] = q[...]
    k[own, :] = kin[:PH, :]
    v[own, :] = vin[:PH, :]
    k[2 * PH :, :] = kin[PH:, :]
    v[2 * PH :, :] = vin[PH:, :]
    dom[:PH, :] = do[:PH, :]
    row = lax.broadcasted_iota(jnp.int32, (R, DH), 0)
    dom[PH:ROWS, :] = jnp.where(row < length, do[PH:, :], jnp.zeros((R, DH), bf))
    kp = lax.broadcasted_iota(jnp.int32, (8, KEYS), 1)
    bias[...] = jnp.where(kp >= offset, 0.0, NEG).astype(f32)
    dkT[...] = jnp.zeros_like(dkT)
    dvT[...] = jnp.zeros_like(dvT)
    for c in kv:
        c.wait_recv()

    NR, NP = R // BQ, PH // BQ
    NX = XR // BQ
    NB = NR + NP + NX - 2 * NX * side
    DPS = (DP0, DP1)

    def info(j):
        resp = j < NR
        extra = (side == 0) & (j >= NR) & (j < NR + NX)
        b = NB - 1 - j
        x = NR + NX - 1 - j
        row0 = jnp.where(resp, PH + (NR - 1 - j) * BQ, jnp.where(extra, ROWS + x * BQ, b * BQ))
        pos0 = jnp.where(resp, PH + row0, jnp.where(extra, 2 * PH - XR + x * BQ, side * PH + row0))
        n = jnp.where(j < NB, lax.div(pos0 + BQ - 1, BK) + 1, 0)
        return pl.multiple_of(jnp.maximum(row0, 0), BQ), pos0, n

    def ks(c):
        return pl.ds(pl.multiple_of(c * BK, BK), BK)

    def scores(slot, row0, pos0, c, masked):
        DP = DPS[slot]
        s = dot_nt(qa[pl.ds(row0, BQ), :], k[ks(c), :])
        dp = dot_nt(dom[pl.ds(row0, BQ), :], v[ks(c), :])
        if masked:
            cols = lax.broadcasted_iota(jnp.int32, (RG, 128), 1)
        for r in range(0, BQ, RG):
            m = mx[r : r + RG, :]
            for i in range(T):
                st = s[r : r + RG, i * 128 : (i + 1) * 128]
                if masked:
                    rows = lax.broadcasted_iota(jnp.int32, (RG, 128), 0) + (pos0 - c * BK + r)
                    ct = cols + i * 128
                    ok = (ct < rows) & (ct + c * BK >= offset) | (ct == rows)
                    st = jnp.where(ok, st, NEG)
                else:
                    st = st + bias[0:1, pl.ds(pl.multiple_of(c * BK + i * 128, 128), 128)]
                S[c * T + i, r : r + RG, :] = st
                m = jnp.maximum(m, st)
                DP[c * T + i, r : r + RG, :] = dp[r : r + RG, i * 128 : (i + 1) * 128]
            mx[r : r + RG, :] = m

    def expo(slot, c):
        DP = DPS[slot]
        for r in range(0, BQ, RG):
            l, tt, m = la[r : r + RG, :], ta[r : r + RG, :], mb[r : r + RG, :]
            for i in range(T):
                e = jnp.exp2(S[c * T + i, r : r + RG, :] * CC - m)
                l = l + e
                tt = tt + e * DP[c * T + i, r : r + RG, :]
                E[c * T + i, r : r + RG, :] = e
            la[r : r + RG, :] = l
            ta[r : r + RG, :] = tt

    def grads_in(slot, c):
        DP = DPS[slot]
        ps, xs = [], []
        for r in range(0, BQ, RG):
            rv, dd = rl[r : r + RG, :], dl[r : r + RG, :]
            pr, xr = [], []
            for i in range(T):
                p = E[c * T + i, r : r + RG, :] * rv
                x = p * (DP[c * T + i, r : r + RG, :] - dd)
                pr.append(p.astype(bf))
                xr.append(x.astype(bf))
            ps.append(jnp.concatenate(pr, 1))
            xs.append(jnp.concatenate(xr, 1))
        return jnp.concatenate(ps, 0), jnp.concatenate(xs, 0)

    def grads_out(c, p, x):
        gv = dot_nn(dT[...], p)
        gk = dot_nn(qT[...], x)
        for i in range(T):
            dvT[c * T + i] += gv[:, i * 128 : (i + 1) * 128]
            dkT[c * T + i] += gk[:, i * 128 : (i + 1) * 128]
        dqa[...] += dot_nn(x, k[ks(c), :])

    def row_max():
        mb[...] = jnp.broadcast_to(jnp.max(mx[...], axis=1, keepdims=True) * CC, (BQ, 128))
        mx[...] = jnp.full((BQ, 128), NEG, f32)

    def row_sums():
        inv = 1.0 / jnp.sum(la[...], axis=1, keepdims=True)
        rl[...] = jnp.broadcast_to(inv, (BQ, 128))
        dl[...] = jnp.broadcast_to(jnp.sum(ta[...], axis=1, keepdims=True) * inv, (BQ, 128))
        la[...] = jnp.zeros((BQ, 128), f32)
        ta[...] = jnp.zeros((BQ, 128), f32)

    def turn(row):
        qT[...] = qa[pl.ds(row, BQ), :].T
        dT[...] = dom[pl.ds(row, BQ), :].T
        dqa[...] = jnp.zeros((BQ, DH), f32)

    def loop(lo, hi, f):
        def body(c, _):
            f(c)
            return 0

        lax.fori_loop(lo, hi, body, 0)

    def feats(a):
        return pl.ds(pl.multiple_of(lax.rem(t + a, NT) * FT, FT), FT)

    def prompt_copy(b, a, h):
        cols = pl.ds(pl.multiple_of(lax.rem(side + b, 2) * PH + h * HP, HP), HP)
        i = b * NT + a
        return pltpu.make_async_remote_copy(
            src_ref=sb.at[feats(a), cols], dst_ref=rb.at[i, :, pl.ds(h * HP, HP)],
            send_sem=p_s.at[h, i], recv_sem=p_r.at[h, i],
            device_id=peer(b, a), device_id_type=MESH,
        )

    def resp_copy(a):
        return pltpu.make_async_remote_copy(
            src_ref=sb.at[feats(a), pl.ds(2 * PH, R)], dst_ref=rr.at[a],
            send_sem=r_s.at[a], recv_sem=r_r.at[a],
            device_id=peer(0, a), device_id_type=MESH,
        )

    def gather(piece, a):
        cols = pl.ds(piece * HP, HP)
        return pltpu.make_async_remote_copy(
            src_ref=ga.at[feats(0), cols], dst_ref=ga.at[feats(0), cols],
            send_sem=g_s.at[piece, a], recv_sem=g_r.at[piece, a],
            device_id=peer(0, a), device_id_type=MESH,
        )

    def pack(c0, tiles):
        def one(i):
            c = c0 + i
            cols = pl.ds(pl.multiple_of(c * 128, 128), 128)
            sb[:DH, cols] = (dkT[c] * SCALE).astype(bf)
            sb[DH:, cols] = dvT[c].astype(bf)

        loop(0, tiles, one)

    HT = HP // 128

    def send_resp():
        pack(2 * PH // 128, R // 128)
        for a in range(1, NT):
            resp_copy(a).start()

    def send_prompt(b, h):
        pack(lax.rem(side + b, 2) * 2 * HT + h * HT, HT)
        for a in range(0 if b else 1, NT):
            prompt_copy(b, a, h).start()

    def finish_resp():
        for a in range(1, NT):
            resp_copy(a).wait_recv()
        for i in range(R // 128):
            cols = slice(i * 128, (i + 1) * 128)
            total = sb[feats(0), 2 * PH + i * 128 : 2 * PH + (i + 1) * 128].astype(f32)
            for a in range(1, NT):
                total = total + rr[a, :, cols].astype(f32)
            ga[feats(0), PH + i * 128 : PH + (i + 1) * 128] = total.astype(bf)
        for a in range(1, NT):
            gather(2, a).start()

    def finish_prompt(h):
        for i in range(1, 2 * NT):
            prompt_copy(i // NT, i % NT, h).wait_recv()
        for c in range(HT):
            cols = slice(h * HP + c * 128, h * HP + (c + 1) * 128)
            mine = pl.ds(pl.multiple_of(side * PH + h * HP + c * 128, 128), 128)
            total = sb[feats(0), mine].astype(f32)
            for i in range(1, 2 * NT):
                total = total + rb[i, :, cols].astype(f32)
            ga[feats(0), cols] = total.astype(bf)
        for a in range(1, NT):
            gather(h, a).start()

    mx[...] = jnp.full((BQ, 128), NEG, f32)
    la[...] = jnp.zeros((BQ, 128), f32)
    ta[...] = jnp.zeros((BQ, 128), f32)
    row_a, pos_a, na = info(jnp.int32(0))
    row_b, pos_b, nb = info(jnp.int32(1))
    loop(0, na - 1, lambda c: scores(0, row_a, pos_a, c, False))
    scores(0, row_a, pos_a, na - 1, True)
    row_max()

    def first(c, masked=False):
        expo(0, c)
        scores(1, row_b, pos_b, c, masked)

    loop(0, nb - 1, first)
    first(nb - 1, True)
    loop(nb, na, lambda c: expo(0, c))
    row_sums()
    row_max()
    turn(row_a)

    def block(j, slot):
        r0, _, n0 = info(j)
        r1, _, n1 = info(j + 1)
        r2, p2, n2 = info(j + 2)

        def three(c, masked=False):
            p, x = grads_in(slot, c)
            expo(1 - slot, c)
            scores(slot, r2, p2, c, masked)
            grads_out(c, p, x)

        def two_of(c):
            p, x = grads_in(slot, c)
            expo(1 - slot, c)
            grads_out(c, p, x)

        def one_of(c):
            grads_out(c, *grads_in(slot, c))

        loop(0, n2 - 1, three)

        @pl.when(n2 > 0)
        def _():
            three(n2 - 1, True)

        loop(n2, n1, two_of)
        loop(n1, n0, one_of)
        @pl.when(r0 < ROWS)
        def _():
            dq[pl.ds(r0, BQ), :] = (dqa[...] * SCALE).astype(bf)

        @pl.when(r0 >= ROWS)
        def _():
            dqx[pl.ds(pl.multiple_of(r0 - ROWS, BQ), BQ), :] = (dqa[...] * SCALE).astype(bf)


        @pl.when(n1 > 0)
        def _():
            row_sums()
            row_max()
            turn(r1)

        @pl.when(j == NR - 1)
        def _():
            send_resp()

        @pl.when((side == 0) & (j == NR + NX - 1))
        def _():
            back.start()
            send_prompt(1, 1)
            send_prompt(1, 0)

        b = NB - 1 - j

        @pl.when(b == NP // 2)
        def _():
            send_prompt(0, 1)

        @pl.when(b == NP // 4)
        def _():
            finish_resp()

    def two(i):
        @pl.when((side == 0) & (i == 1))
        def _():
            for c in over:
                c.wait_recv()

        block(2 * i, 0)
        block(2 * i + 1, 1)

    loop(0, lax.div(NB, 2), two)

    @pl.when(side == 1)
    def _():
        send_prompt(1, 1)
        send_prompt(1, 0)

    send_prompt(0, 0)
    finish_prompt(1)
    finish_prompt(0)

    @pl.when(side == 0)
    def _():
        back.wait_send()

    @pl.when(side == 1)
    def _():
        back.wait_recv()
        for c in over:
            c.wait_send()

    for c in kv:
        c.wait_send()
    for i in range(1, 2 * NT):
        for h in range(2):
            prompt_copy(i // NT, i % NT, h).wait_send()
    for a in range(1, NT):
        resp_copy(a).wait_send()
    for piece in (2, 1, 0):
        for a in range(1, NT):
            gather(piece, a).wait()
        for c in range(piece * HP, (piece + 1) * HP, 256):
            dk[c : c + 256, :] = ga[:DH, c : c + 256].T
            dv[c : c + 256, :] = ga[DH:, c : c + 256].T


def per_device(queries, keys, values, dout, offsets, lengths):
    V = pl.BlockSpec(memory_space=pltpu.VMEM)
    SM = pl.BlockSpec(memory_space=pltpu.SMEM)
    D = pltpu.SemaphoreType.DMA
    big = pltpu.VMEM((KEYS // 128, BQ, 128), f32)
    acc = pltpu.VMEM((KEYS // 128, DH, 128), f32)
    stat = pltpu.VMEM((BQ, 128), f32)
    return tuple(
        pl.pallas_call(
            kernel,
            out_shape=[jax.ShapeDtypeStruct((ROWS, DH), bf)] * 3,
            in_specs=[SM, SM, V, V, V, V],
            out_specs=[V, V, V],
            scratch_shapes=[
                pltpu.VMEM((KEYS, DH), bf), pltpu.VMEM((KEYS, DH), bf),
                acc, acc, big, big, big, big,
                stat, stat, stat, stat, stat, stat,
                pltpu.VMEM((BQ, DH), f32), pltpu.VMEM((ROWS + XR, DH), bf),
                pltpu.VMEM((DH, BQ), bf), pltpu.VMEM((DH, BQ), bf),
                pltpu.VMEM((8, KEYS), f32),
                pltpu.VMEM((ROWS + XR, DH), bf), pltpu.VMEM((XR, DH), bf),
                pltpu.VMEM((2 * DH, KEYS), bf), pltpu.VMEM((2 * NT, FT, PH), bf),
                pltpu.VMEM((NT, FT, R), bf), pltpu.VMEM((2 * DH, ROWS), bf),
                D((4,)), D((4,)), D((2, 2 * NT)), D((2, 2 * NT)), D((NT,)), D((NT,)),
                D((3, NT)), D((3, NT)), D((3,)), D((3,)),
            ],
            compiler_params=pltpu.CompilerParams(
                collective_id=0, has_side_effects=True, vmem_limit_bytes=60 * 2**20
            ),
        )(offsets, lengths, queries, keys, values, dout)
    )


def solution(mesh):
    return jax.shard_map(
        per_device,
        mesh=mesh,
        in_specs=(P("dp", "tensor"), P("dp", None), P("dp", None), P("dp", "tensor"), P(), P("dp")),
        out_specs=(P("dp", "tensor"), P("dp", None), P("dp", None)),
        check_vma=False,
    )
```

```python
import functools

import jax
import jax.numpy as jnp
from jax import lax
from jax.experimental import pallas as pl
from jax.experimental.pallas import tpu as pltpu
from jax.sharding import PartitionSpec as P

MESH = pl.DeviceIdType.MESH
f32 = jnp.float32
bf = jnp.bfloat16

PH = 2048
R = 1024
DH = 128
KEYS = 2 * PH + R
BQ, BK = 256, 512
RG = 16
T = BK // 128
NT = 8
FT = 2 * DH // NT
NPC = 4
PC = PH // NPC
HP = PH // 2
XR = 768
ROWS = PH + R
NEG = -1e30
EARLY = (3,)
SCALE = 1.0 / DH**0.5
CC = SCALE * 1.4426950408889634


def dot_nt(a, b):
    return lax.dot_general(a, b, (((1,), (1,)), ((), ())), preferred_element_type=f32)


def dot_nn(a, b):
    return jnp.dot(a, b, preferred_element_type=f32)


def kernel(
    offs, lens, q, kin, vin, do, dq, dk, dv,
    k, v, dkT, dvT, S, E, DP0, DP1, mx, mb, la, ta, rl, dl, dqa, dom, qT, dT, bias,
    qa, dqx, sb, rb, rr, ga,
    kv_s, kv_r, p_s, p_r, r_s, r_r, g_s, g_r, x_s, x_r,
):
    d = lax.axis_index("dp")
    t = lax.axis_index("tensor")
    half = lax.axis_size("dp") // 2
    side = lax.div(d, half)
    pair = lax.rem(d, half)
    offset = offs[pair]
    length = lens[0]

    def peer(b, a):
        return (lax.rem(side + b, 2) * half + pair, lax.rem(t + a, NT))

    barrier = pltpu.get_barrier_semaphore()
    for i in range(1, 2 * NT):
        pl.semaphore_signal(barrier, inc=1, device_id=peer(i // NT, i % NT), device_id_type=MESH)
    pl.semaphore_wait(barrier, 2 * NT - 1)

    flip = t + 1 - 2 * lax.rem(t, 2)
    kv = []
    for h in range(2):
        dst = (lax.rem(side + 1, 2) * half + pair, t if h == 0 else flip)
        for i, (src, to) in enumerate(((kin, k), (vin, v))):
            rows = pl.ds(pl.multiple_of(side * PH + h * HP, HP), HP)
            c = pltpu.make_async_remote_copy(
                src_ref=src.at[pl.ds(h * HP, HP)], dst_ref=to.at[rows],
                send_sem=kv_s.at[2 * h + i], recv_sem=kv_r.at[2 * h + i],
                device_id=dst, device_id_type=MESH,
            )
            c.start()
            kv.append(c)

    over = [
        pltpu.make_async_remote_copy(
            src_ref=src.at[pl.ds(PH - XR, XR)], dst_ref=to.at[pl.ds(ROWS, XR)],
            send_sem=x_s.at[i], recv_sem=x_r.at[i], device_id=peer(1, 0), device_id_type=MESH,
        )
        for i, (src, to) in enumerate(((q, qa), (do, dom)))
    ]
    back = pltpu.make_async_remote_copy(
        src_ref=dqx, dst_ref=dq.at[pl.ds(PH - XR, XR)],
        send_sem=x_s.at[2], recv_sem=x_r.at[2], device_id=peer(1, 0), device_id_type=MESH,
    )

    @pl.when(side == 1)
    def _():
        for c in over:
            c.start()

    own = pl.ds(pl.multiple_of(side * PH, PH), PH)
    qa[:ROWS, :] = q[...]
    k[own, :] = kin[:PH, :]
    v[own, :] = vin[:PH, :]
    k[2 * PH :, :] = kin[PH:, :]
    v[2 * PH :, :] = vin[PH:, :]
    dom[:PH, :] = do[:PH, :]
    row = lax.broadcasted_iota(jnp.int32, (R, DH), 0)
    dom[PH:ROWS, :] = jnp.where(row < length, do[PH:, :], jnp.zeros((R, DH), bf))
    kp = lax.broadcasted_iota(jnp.int32, (8, KEYS), 1)
    bias[...] = jnp.where(kp >= offset, 0.0, NEG).astype(f32)
    dkT[...] = jnp.zeros_like(dkT)
    dvT[...] = jnp.zeros_like(dvT)
    for c in kv:
        c.wait_recv()

    NR, NP = R // BQ, PH // BQ
    NX = XR // BQ
    NB = NR + NP + NX - 2 * NX * side
    DPS = (DP0, DP1)

    def info(j):
        resp = j < NR
        extra = (side == 0) & (j >= NR) & (j < NR + NX)
        b = NB - 1 - j
        x = NR + NX - 1 - j
        row0 = jnp.where(resp, PH + (NR - 1 - j) * BQ, jnp.where(extra, ROWS + x * BQ, b * BQ))
        pos0 = jnp.where(resp, PH + row0, jnp.where(extra, 2 * PH - XR + x * BQ, side * PH + row0))
        n = jnp.where(j < NB, lax.div(pos0 + BQ - 1, BK) + 1, 0)
        return pl.multiple_of(jnp.maximum(row0, 0), BQ), pos0, n

    def ks(c):
        return pl.ds(pl.multiple_of(c * BK, BK), BK)

    def scores(slot, row0, pos0, c, masked):
        DP = DPS[slot]
        s = dot_nt(qa[pl.ds(row0, BQ), :], k[ks(c), :])
        dp = dot_nt(dom[pl.ds(row0, BQ), :], v[ks(c), :])
        if masked:
            cols = lax.broadcasted_iota(jnp.int32, (RG, 128), 1)
        for r in range(0, BQ, RG):
            m = mx[r : r + RG, :]
            for i in range(T):
                st = s[r : r + RG, i * 128 : (i + 1) * 128]
                if masked:
                    rows = lax.broadcasted_iota(jnp.int32, (RG, 128), 0) + (pos0 - c * BK + r)
                    ct = cols + i * 128
                    ok = (ct < rows) & (ct + c * BK >= offset) | (ct == rows)
                    st = jnp.where(ok, st, NEG)
                else:
                    st = st + bias[0:1, pl.ds(pl.multiple_of(c * BK + i * 128, 128), 128)]
                S[c * T + i, r : r + RG, :] = st
                m = jnp.maximum(m, st)
                DP[c * T + i, r : r + RG, :] = dp[r : r + RG, i * 128 : (i + 1) * 128]
            mx[r : r + RG, :] = m

    def expo(slot, c):
        DP = DPS[slot]
        for r in range(0, BQ, RG):
            l, tt, m = la[r : r + RG, :], ta[r : r + RG, :], mb[r : r + RG, :]
            for i in range(T):
                e = jnp.exp2(S[c * T + i, r : r + RG, :] * CC - m)
                l = l + e
                tt = tt + e * DP[c * T + i, r : r + RG, :]
                E[c * T + i, r : r + RG, :] = e
            la[r : r + RG, :] = l
            ta[r : r + RG, :] = tt

    def grads_in(slot, c):
        DP = DPS[slot]
        ps, xs = [], []
        for r in range(0, BQ, RG):
            rv, dd = rl[r : r + RG, :], dl[r : r + RG, :]
            pr, xr = [], []
            for i in range(T):
                p = E[c * T + i, r : r + RG, :] * rv
                x = p * (DP[c * T + i, r : r + RG, :] - dd)
                pr.append(p.astype(bf))
                xr.append(x.astype(bf))
            ps.append(jnp.concatenate(pr, 1))
            xs.append(jnp.concatenate(xr, 1))
        return jnp.concatenate(ps, 0), jnp.concatenate(xs, 0)

    def grads_out(c, p, x):
        gv = dot_nn(dT[...], p)
        gk = dot_nn(qT[...], x)
        for i in range(T):
            dvT[c * T + i] += gv[:, i * 128 : (i + 1) * 128]
            dkT[c * T + i] += gk[:, i * 128 : (i + 1) * 128]
        dqa[...] += dot_nn(x, k[ks(c), :])

    def row_max():
        mb[...] = jnp.broadcast_to(jnp.max(mx[...], axis=1, keepdims=True) * CC, (BQ, 128))
        mx[...] = jnp.full((BQ, 128), NEG, f32)

    def row_sums():
        inv = 1.0 / jnp.sum(la[...], axis=1, keepdims=True)
        rl[...] = jnp.broadcast_to(inv, (BQ, 128))
        dl[...] = jnp.broadcast_to(jnp.sum(ta[...], axis=1, keepdims=True) * inv, (BQ, 128))
        la[...] = jnp.zeros((BQ, 128), f32)
        ta[...] = jnp.zeros((BQ, 128), f32)

    def turn(row):
        qT[...] = qa[pl.ds(row, BQ), :].T
        dT[...] = dom[pl.ds(row, BQ), :].T
        dqa[...] = jnp.zeros((BQ, DH), f32)

    def loop(lo, hi, f):
        def body(c, _):
            f(c)
            return 0

        lax.fori_loop(lo, hi, body, 0)

    def feats(a):
        return pl.ds(pl.multiple_of(lax.rem(t + a, NT) * FT, FT), FT)

    def prompt_copy(b, a, h):
        cols = pl.ds(pl.multiple_of(lax.rem(side + b, 2) * PH + h * PC, PC), PC)
        i = b * NT + a
        return pltpu.make_async_remote_copy(
            src_ref=sb.at[feats(a), cols], dst_ref=rb.at[i, :, pl.ds(h * PC, PC)],
            send_sem=p_s.at[h, i], recv_sem=p_r.at[h, i],
            device_id=peer(b, a), device_id_type=MESH,
        )

    def resp_copy(a):
        return pltpu.make_async_remote_copy(
            src_ref=sb.at[feats(a), pl.ds(2 * PH, R)], dst_ref=rr.at[a],
            send_sem=r_s.at[a], recv_sem=r_r.at[a],
            device_id=peer(0, a), device_id_type=MESH,
        )

    def gather(piece, a):
        cols = pl.ds(piece * PC, PC if piece < NPC else R)
        return pltpu.make_async_remote_copy(
            src_ref=ga.at[feats(0), cols], dst_ref=ga.at[feats(0), cols],
            send_sem=g_s.at[piece, a], recv_sem=g_r.at[piece, a],
            device_id=peer(0, a), device_id_type=MESH,
        )

    def pack(c0, tiles):
        def one(i):
            c = c0 + i
            cols = pl.ds(pl.multiple_of(c * 128, 128), 128)
            sb[:DH, cols] = (dkT[c] * SCALE).astype(bf)
            sb[DH:, cols] = dvT[c].astype(bf)

        loop(0, tiles, one)

    HT = PC // 128

    def send_resp():
        pack(2 * PH // 128, R // 128)
        for a in range(1, NT):
            resp_copy(a).start()

    def send_prompt(b, h):
        pack(lax.rem(side + b, 2) * NPC * HT + h * HT, HT)
        for a in range(0 if b else 1, NT):
            prompt_copy(b, a, h).start()

    def finish_resp():
        for a in range(1, NT):
            resp_copy(a).wait_recv()
        for i in range(R // 128):
            cols = slice(i * 128, (i + 1) * 128)
            total = sb[feats(0), 2 * PH + i * 128 : 2 * PH + (i + 1) * 128].astype(f32)
            for a in range(1, NT):
                total = total + rr[a, :, cols].astype(f32)
            ga[feats(0), PH + i * 128 : PH + (i + 1) * 128] = total.astype(bf)
        for a in range(1, NT):
            gather(NPC, a).start()

    def finish_prompt(h):
        for i in range(1, 2 * NT):
            prompt_copy(i // NT, i % NT, h).wait_recv()
        for c in range(HT):
            cols = slice(h * PC + c * 128, h * PC + (c + 1) * 128)
            mine = pl.ds(pl.multiple_of(side * PH + h * PC + c * 128, 128), 128)
            total = sb[feats(0), mine].astype(f32)
            for i in range(1, 2 * NT):
                total = total + rb[i, :, cols].astype(f32)
            ga[feats(0), cols] = total.astype(bf)
        for a in range(1, NT):
            gather(h, a).start()

    mx[...] = jnp.full((BQ, 128), NEG, f32)
    la[...] = jnp.zeros((BQ, 128), f32)
    ta[...] = jnp.zeros((BQ, 128), f32)
    row_a, pos_a, na = info(jnp.int32(0))
    row_b, pos_b, nb = info(jnp.int32(1))
    loop(0, na - 1, lambda c: scores(0, row_a, pos_a, c, False))
    scores(0, row_a, pos_a, na - 1, True)
    row_max()

    def first(c, masked=False):
        expo(0, c)
        scores(1, row_b, pos_b, c, masked)

    loop(0, nb - 1, first)
    first(nb - 1, True)
    loop(nb, na, lambda c: expo(0, c))
    row_sums()
    row_max()
    turn(row_a)

    def block(j, slot):
        r0, _, n0 = info(j)
        r1, _, n1 = info(j + 1)
        r2, p2, n2 = info(j + 2)

        def three(c, masked=False):
            p, x = grads_in(slot, c)
            expo(1 - slot, c)
            scores(slot, r2, p2, c, masked)
            grads_out(c, p, x)

        def two_of(c):
            p, x = grads_in(slot, c)
            expo(1 - slot, c)
            grads_out(c, p, x)

        def one_of(c):
            grads_out(c, *grads_in(slot, c))

        loop(0, n2 - 1, three)

        @pl.when(n2 > 0)
        def _():
            three(n2 - 1, True)

        loop(n2, n1, two_of)
        loop(n1, n0, one_of)
        @pl.when((r0 < ROWS) & (n0 > 0))
        def _():
            dq[pl.ds(r0, BQ), :] = (dqa[...] * SCALE).astype(bf)

        @pl.when(r0 >= ROWS)
        def _():
            dqx[pl.ds(pl.multiple_of(r0 - ROWS, BQ), BQ), :] = (dqa[...] * SCALE).astype(bf)


        @pl.when(n1 > 0)
        def _():
            row_sums()
            row_max()
            turn(r1)

        @pl.when(j == NR - 1)
        def _():
            send_resp()

            @pl.when(side == 1)
            def _():
                for h in range(-((NX - NP) // 2), NPC):
                    send_prompt(0, h)

        @pl.when((side == 0) & (j == NR + NX - 1))
        def _():
            back.start()
            for h in range(NPC - 1, -1, -1):
                send_prompt(1, h)

        @pl.when(j == NR + 1)
        def _():
            finish_resp()

        b = NB - 1 - j
        for h in range(1, NPC):

            @pl.when((b == 2 * h) & (j >= NR + NX - NX * side))
            def _():
                send_prompt(0, h)

        @pl.when((side == 0) & (b == 1))
        def _():
            for h in EARLY:
                finish_prompt(h)

    def two(i):
        @pl.when((side == 0) & (i == 1))
        def _():
            for c in over:
                c.wait_recv()

        block(2 * i, 0)
        block(2 * i + 1, 1)

    loop(0, lax.div(NB + 1, 2), two)

    @pl.when(side == 1)
    def _():
        for h in range(NPC - 1, -1, -1):
            send_prompt(1, h)

    send_prompt(0, 0)

    @pl.when(side == 1)
    def _():
        for h in EARLY:
            finish_prompt(h)

    for h in range(NPC - 1, -1, -1):
        if h not in EARLY:
            finish_prompt(h)

    @pl.when(side == 0)
    def _():
        back.wait_send()

    @pl.when(side == 1)
    def _():
        back.wait_recv()
        for c in over:
            c.wait_send()

    for c in kv:
        c.wait_send()
    for i in range(1, 2 * NT):
        for h in range(NPC):
            prompt_copy(i // NT, i % NT, h).wait_send()
    for a in range(1, NT):
        resp_copy(a).wait_send()
    for piece in range(NPC, -1, -1):
        for a in range(1, NT):
            gather(piece, a).wait()
        for c in range(piece * PC, ROWS if piece == NPC else (piece + 1) * PC, 256):
            dk[c : c + 256, :] = ga[:DH, c : c + 256].T
            dv[c : c + 256, :] = ga[DH:, c : c + 256].T


def per_device(queries, keys, values, dout, offsets, lengths):
    V = pl.BlockSpec(memory_space=pltpu.VMEM)
    SM = pl.BlockSpec(memory_space=pltpu.SMEM)
    D = pltpu.SemaphoreType.DMA
    big = pltpu.VMEM((KEYS // 128, BQ, 128), f32)
    acc = pltpu.VMEM((KEYS // 128, DH, 128), f32)
    stat = pltpu.VMEM((BQ, 128), f32)
    return tuple(
        pl.pallas_call(
            kernel,
            out_shape=[jax.ShapeDtypeStruct((ROWS, DH), bf)] * 3,
            in_specs=[SM, SM, V, V, V, V],
            out_specs=[V, V, V],
            scratch_shapes=[
                pltpu.VMEM((KEYS, DH), bf), pltpu.VMEM((KEYS, DH), bf),
                acc, acc, big, big, big, big,
                stat, stat, stat, stat, stat, stat,
                pltpu.VMEM((BQ, DH), f32), pltpu.VMEM((ROWS + XR, DH), bf),
                pltpu.VMEM((DH, BQ), bf), pltpu.VMEM((DH, BQ), bf),
                pltpu.VMEM((8, KEYS), f32),
                pltpu.VMEM((ROWS + XR, DH), bf), pltpu.VMEM((XR, DH), bf),
                pltpu.VMEM((2 * DH, KEYS), bf), pltpu.VMEM((2 * NT, FT, PH), bf),
                pltpu.VMEM((NT, FT, R), bf), pltpu.VMEM((2 * DH, ROWS), bf),
                D((4,)), D((4,)), D((NPC, 2 * NT)), D((NPC, 2 * NT)), D((NT,)), D((NT,)),
                D((NPC + 1, NT)), D((NPC + 1, NT)), D((3,)), D((3,)),
            ],
            compiler_params=pltpu.CompilerParams(
                collective_id=0, has_side_effects=True, vmem_limit_bytes=60 * 2**20
            ),
        )(offsets, lengths, queries, keys, values, dout)
    )


def solution(mesh):
    return jax.shard_map(
        per_device,
        mesh=mesh,
        in_specs=(P("dp", "tensor"), P("dp", None), P("dp", None), P("dp", "tensor"), P(), P("dp")),
        out_specs=(P("dp", "tensor"), P("dp", None), P("dp", None)),
        check_vma=False,
    )
```

```python
import functools

import jax
import jax.numpy as jnp
from jax import lax
from jax.experimental import pallas as pl
from jax.experimental.pallas import tpu as pltpu
from jax.sharding import PartitionSpec as P

MESH = pl.DeviceIdType.MESH
f32 = jnp.float32
bf = jnp.bfloat16

PH = 2048
R = 1024
DH = 128
KEYS = 2 * PH + R
BQ, BK = 256, 512
RG = 16
T = BK // 128
NT = 8
FT = 2 * DH // NT
NPC = 4
PC = PH // NPC
HP = PH // 2
XR = 768
ROWS = PH + R
NEG = -1e30
EARLY = (3,)
SCALE = 1.0 / DH**0.5
CC = SCALE * 1.4426950408889634


def dot_nt(a, b):
    return lax.dot_general(a, b, (((1,), (1,)), ((), ())), preferred_element_type=f32)


def dot_nn(a, b):
    return jnp.dot(a, b, preferred_element_type=f32)


def kernel(
    offs, lens, q, kin, vin, do, dq, dk, dv,
    k, v, dkT, dvT, S, E, DP0, DP1, mx, mb, la, ta, rl, dl, dqa, dom, qT, dT, bias,
    qa, dqx, sb, rb, rr, ga,
    kv_s, kv_r, p_s, p_r, r_s, r_r, g_s, g_r, x_s, x_r, l_s,
):
    d = lax.axis_index("dp")
    t = lax.axis_index("tensor")
    half = lax.axis_size("dp") // 2
    side = lax.div(d, half)
    pair = lax.rem(d, half)
    offset = offs[pair]
    length = lens[0]

    def peer(b, a):
        return (lax.rem(side + b, 2) * half + pair, lax.rem(t + a, NT))

    own = pl.ds(pl.multiple_of(side * PH, PH), PH)
    loads = [
        pltpu.make_async_copy(src, dst, l_s.at[i])
        for i, (src, dst) in enumerate((
            (kin.at[pl.ds(0, PH)], k.at[own]), (kin.at[pl.ds(PH, R)], k.at[pl.ds(2 * PH, R)]),
            (vin.at[pl.ds(0, PH)], v.at[own]), (vin.at[pl.ds(PH, R)], v.at[pl.ds(2 * PH, R)]),
            (q, qa.at[pl.ds(0, ROWS)]), (do, dom.at[pl.ds(0, ROWS)]),
        ))
    ]
    for c in loads:
        c.start()

    barrier = pltpu.get_barrier_semaphore()
    for i in range(1, 2 * NT):
        pl.semaphore_signal(barrier, inc=1, device_id=peer(i // NT, i % NT), device_id_type=MESH)
    pl.semaphore_wait(barrier, 2 * NT - 1)

    flip = t + 1 - 2 * lax.rem(t, 2)
    kv = []
    for h in range(2):
        dst = (lax.rem(side + 1, 2) * half + pair, t if h == 0 else flip)
        for i, (src, to) in enumerate(((kin, k), (vin, v))):
            rows = pl.ds(pl.multiple_of(side * PH + h * HP, HP), HP)
            c = pltpu.make_async_remote_copy(
                src_ref=src.at[pl.ds(h * HP, HP)], dst_ref=to.at[rows],
                send_sem=kv_s.at[2 * h + i], recv_sem=kv_r.at[2 * h + i],
                device_id=dst, device_id_type=MESH,
            )
            c.start()
            kv.append(c)

    over = [
        pltpu.make_async_remote_copy(
            src_ref=src.at[pl.ds(PH - XR, XR)], dst_ref=to.at[pl.ds(ROWS, XR)],
            send_sem=x_s.at[i], recv_sem=x_r.at[i], device_id=peer(1, 0), device_id_type=MESH,
        )
        for i, (src, to) in enumerate(((q, qa), (do, dom)))
    ]
    back = pltpu.make_async_remote_copy(
        src_ref=dqx, dst_ref=dq.at[pl.ds(PH - XR, XR)],
        send_sem=x_s.at[2], recv_sem=x_r.at[2], device_id=peer(1, 0), device_id_type=MESH,
    )

    @pl.when(side == 1)
    def _():
        for c in over:
            c.start()

    kp = lax.broadcasted_iota(jnp.int32, (8, KEYS), 1)
    bias[...] = jnp.where(kp >= offset, 0.0, NEG).astype(f32)
    dkT[...] = jnp.zeros_like(dkT)
    dvT[...] = jnp.zeros_like(dvT)
    for c in loads:
        c.wait()
    row = lax.broadcasted_iota(jnp.int32, (R, DH), 0)
    dom[PH:ROWS, :] = jnp.where(row < length, dom[PH:ROWS, :], jnp.zeros((R, DH), bf))

    NR, NP = R // BQ, PH // BQ
    NX = XR // BQ
    NB = NR + NP + NX - 2 * NX * side
    DPS = (DP0, DP1)

    def info(j):
        resp = j < NR
        extra = (side == 0) & (j >= NR) & (j < NR + NX)
        b = NB - 1 - j
        x = NR + NX - 1 - j
        row0 = jnp.where(resp, PH + (NR - 1 - j) * BQ, jnp.where(extra, ROWS + x * BQ, b * BQ))
        pos0 = jnp.where(resp, PH + row0, jnp.where(extra, 2 * PH - XR + x * BQ, side * PH + row0))
        n = jnp.where(j < NB, lax.div(pos0 + BQ - 1, BK) + 1, 0)
        return pl.multiple_of(jnp.maximum(row0, 0), BQ), pos0, n

    def ks(c):
        return pl.ds(pl.multiple_of(c * BK, BK), BK)

    def scores(slot, row0, pos0, c, masked):
        DP = DPS[slot]
        s = dot_nt(qa[pl.ds(row0, BQ), :], k[ks(c), :])
        dp = dot_nt(dom[pl.ds(row0, BQ), :], v[ks(c), :])
        if masked:
            cols = lax.broadcasted_iota(jnp.int32, (RG, 128), 1)
        for r in range(0, BQ, RG):
            m = mx[r : r + RG, :]
            for i in range(T):
                st = s[r : r + RG, i * 128 : (i + 1) * 128]
                if masked:
                    rows = lax.broadcasted_iota(jnp.int32, (RG, 128), 0) + (pos0 - c * BK + r)
                    ct = cols + i * 128
                    ok = (ct < rows) & (ct + c * BK >= offset) | (ct == rows)
                    st = jnp.where(ok, st, NEG)
                else:
                    st = st + bias[0:1, pl.ds(pl.multiple_of(c * BK + i * 128, 128), 128)]
                S[c * T + i, r : r + RG, :] = st
                m = jnp.maximum(m, st)
                DP[c * T + i, r : r + RG, :] = dp[r : r + RG, i * 128 : (i + 1) * 128]
            mx[r : r + RG, :] = m

    def expo(slot, c):
        DP = DPS[slot]
        for r in range(0, BQ, RG):
            l, tt, m = la[r : r + RG, :], ta[r : r + RG, :], mb[r : r + RG, :]
            for i in range(T):
                e = jnp.exp2(S[c * T + i, r : r + RG, :] * CC - m)
                l = l + e
                tt = tt + e * DP[c * T + i, r : r + RG, :]
                E[c * T + i, r : r + RG, :] = e
            la[r : r + RG, :] = l
            ta[r : r + RG, :] = tt

    def grads_in(slot, c):
        DP = DPS[slot]
        ps, xs = [], []
        for r in range(0, BQ, RG):
            rv, dd = rl[r : r + RG, :], dl[r : r + RG, :]
            pr, xr = [], []
            for i in range(T):
                p = E[c * T + i, r : r + RG, :] * rv
                x = p * (DP[c * T + i, r : r + RG, :] - dd)
                pr.append(p.astype(bf))
                xr.append(x.astype(bf))
            ps.append(jnp.concatenate(pr, 1))
            xs.append(jnp.concatenate(xr, 1))
        return jnp.concatenate(ps, 0), jnp.concatenate(xs, 0)

    def grads_out(c, p, x):
        gv = dot_nn(dT[...], p)
        gk = dot_nn(qT[...], x)
        for i in range(T):
            dvT[c * T + i] += gv[:, i * 128 : (i + 1) * 128]
            dkT[c * T + i] += gk[:, i * 128 : (i + 1) * 128]
        dqa[...] += dot_nn(x, k[ks(c), :])

    def row_max():
        mb[...] = jnp.broadcast_to(jnp.max(mx[...], axis=1, keepdims=True) * CC, (BQ, 128))
        mx[...] = jnp.full((BQ, 128), NEG, f32)

    def row_sums():
        inv = 1.0 / jnp.sum(la[...], axis=1, keepdims=True)
        rl[...] = jnp.broadcast_to(inv, (BQ, 128))
        dl[...] = jnp.broadcast_to(jnp.sum(ta[...], axis=1, keepdims=True) * inv, (BQ, 128))
        la[...] = jnp.zeros((BQ, 128), f32)
        ta[...] = jnp.zeros((BQ, 128), f32)

    def turn(row):
        qT[...] = qa[pl.ds(row, BQ), :].T
        dT[...] = dom[pl.ds(row, BQ), :].T
        dqa[...] = jnp.zeros((BQ, DH), f32)

    def loop(lo, hi, f):
        def body(c, _):
            f(c)
            return 0

        lax.fori_loop(lo, hi, body, 0)

    def feats(a):
        return pl.ds(pl.multiple_of(lax.rem(t + a, NT) * FT, FT), FT)

    def prompt_copy(b, a, h):
        cols = pl.ds(pl.multiple_of(lax.rem(side + b, 2) * PH + h * PC, PC), PC)
        i = b * NT + a
        return pltpu.make_async_remote_copy(
            src_ref=sb.at[feats(a), cols], dst_ref=rb.at[i, :, pl.ds(h * PC, PC)],
            send_sem=p_s.at[h, i], recv_sem=p_r.at[h, i],
            device_id=peer(b, a), device_id_type=MESH,
        )

    def resp_copy(a):
        return pltpu.make_async_remote_copy(
            src_ref=sb.at[feats(a), pl.ds(2 * PH, R)], dst_ref=rr.at[a],
            send_sem=r_s.at[a], recv_sem=r_r.at[a],
            device_id=peer(0, a), device_id_type=MESH,
        )

    def gather(piece, a):
        cols = pl.ds(piece * PC, PC if piece < NPC else R)
        return pltpu.make_async_remote_copy(
            src_ref=ga.at[feats(0), cols], dst_ref=ga.at[feats(0), cols],
            send_sem=g_s.at[piece, a], recv_sem=g_r.at[piece, a],
            device_id=peer(0, a), device_id_type=MESH,
        )

    def pack(c0, tiles):
        def one(i):
            c = c0 + i
            cols = pl.ds(pl.multiple_of(c * 128, 128), 128)
            sb[:DH, cols] = (dkT[c] * SCALE).astype(bf)
            sb[DH:, cols] = dvT[c].astype(bf)

        loop(0, tiles, one)

    HT = PC // 128

    def send_resp():
        pack(2 * PH // 128, R // 128)
        for a in range(1, NT):
            resp_copy(a).start()

    def send_prompt(b, h):
        pack(lax.rem(side + b, 2) * NPC * HT + h * HT, HT)
        for a in range(0 if b else 1, NT):
            prompt_copy(b, a, h).start()

    def finish_resp():
        for a in range(1, NT):
            resp_copy(a).wait_recv()
        for i in range(R // 128):
            cols = slice(i * 128, (i + 1) * 128)
            total = sb[feats(0), 2 * PH + i * 128 : 2 * PH + (i + 1) * 128].astype(f32)
            for a in range(1, NT):
                total = total + rr[a, :, cols].astype(f32)
            ga[feats(0), PH + i * 128 : PH + (i + 1) * 128] = total.astype(bf)
        for a in range(1, NT):
            gather(NPC, a).start()

    def finish_prompt(h):
        for i in range(1, 2 * NT):
            prompt_copy(i // NT, i % NT, h).wait_recv()
        for c in range(HT):
            cols = slice(h * PC + c * 128, h * PC + (c + 1) * 128)
            mine = pl.ds(pl.multiple_of(side * PH + h * PC + c * 128, 128), 128)
            total = sb[feats(0), mine].astype(f32)
            for i in range(1, 2 * NT):
                total = total + rb[i, :, cols].astype(f32)
            ga[feats(0), cols] = total.astype(bf)
        for a in range(1, NT):
            gather(h, a).start()

    mx[...] = jnp.full((BQ, 128), NEG, f32)
    la[...] = jnp.zeros((BQ, 128), f32)
    ta[...] = jnp.zeros((BQ, 128), f32)
    row_a, pos_a, na = info(jnp.int32(0))
    row_b, pos_b, nb = info(jnp.int32(1))
    PB = PH // BK
    loop(side * PB, side * PB + PB, lambda c: scores(0, row_a, pos_a, c, False))
    loop(2 * PB, na - 1, lambda c: scores(0, row_a, pos_a, c, False))
    scores(0, row_a, pos_a, na - 1, True)
    for c in kv:
        c.wait_recv()
    loop(PB - side * PB, 2 * PB - side * PB, lambda c: scores(0, row_a, pos_a, c, False))
    row_max()

    def first(c, masked=False):
        expo(0, c)
        scores(1, row_b, pos_b, c, masked)

    loop(0, nb - 1, first)
    first(nb - 1, True)
    loop(nb, na, lambda c: expo(0, c))
    row_sums()
    row_max()
    turn(row_a)

    def block(j, slot):
        r0, _, n0 = info(j)
        r1, _, n1 = info(j + 1)
        r2, p2, n2 = info(j + 2)

        def three(c, masked=False):
            p, x = grads_in(slot, c)
            expo(1 - slot, c)
            scores(slot, r2, p2, c, masked)
            grads_out(c, p, x)

        def two_of(c):
            p, x = grads_in(slot, c)
            expo(1 - slot, c)
            grads_out(c, p, x)

        def one_of(c):
            grads_out(c, *grads_in(slot, c))

        loop(0, n2 - 1, three)

        @pl.when(n2 > 0)
        def _():
            three(n2 - 1, True)

        loop(n2, n1, two_of)
        loop(n1, n0, one_of)
        @pl.when((r0 < ROWS) & (n0 > 0))
        def _():
            dq[pl.ds(r0, BQ), :] = (dqa[...] * SCALE).astype(bf)

        @pl.when(r0 >= ROWS)
        def _():
            dqx[pl.ds(pl.multiple_of(r0 - ROWS, BQ), BQ), :] = (dqa[...] * SCALE).astype(bf)


        @pl.when(n1 > 0)
        def _():
            row_sums()
            row_max()
            turn(r1)

        @pl.when(j == NR - 1)
        def _():
            send_resp()

            @pl.when(side == 1)
            def _():
                for h in range(-((NX - NP) // 2), NPC):
                    send_prompt(0, h)

        @pl.when((side == 0) & (j == NR + NX - 1))
        def _():
            back.start()
            for h in range(NPC - 1, -1, -1):
                send_prompt(1, h)

        @pl.when(j == NR + 1)
        def _():
            finish_resp()

        b = NB - 1 - j
        for h in range(1, NPC):

            @pl.when((b == 2 * h) & (j >= NR + NX - NX * side))
            def _():
                send_prompt(0, h)

        @pl.when((side == 0) & (b == 1))
        def _():
            for h in EARLY:
                finish_prompt(h)

    def two(i):
        @pl.when((side == 0) & (i == 1))
        def _():
            for c in over:
                c.wait_recv()

        block(2 * i, 0)
        block(2 * i + 1, 1)

    loop(0, lax.div(NB + 1, 2), two)

    @pl.when(side == 1)
    def _():
        for h in range(NPC - 1, -1, -1):
            send_prompt(1, h)

    send_prompt(0, 0)

    @pl.when(side == 1)
    def _():
        for h in range(NPC):
            for a in range(NT):
                prompt_copy(1, a, h).wait_send()
        for h in EARLY:
            finish_prompt(h)

    for h in range(NPC - 1, -1, -1):
        if h not in EARLY:
            finish_prompt(h)

    @pl.when(side == 0)
    def _():
        back.wait_send()

    @pl.when(side == 1)
    def _():
        back.wait_recv()
        for c in over:
            c.wait_send()

    for c in kv:
        c.wait_send()
    for h in range(NPC):
        for a in range(1, NT):
            prompt_copy(0, a, h).wait_send()

        @pl.when(side == 0)
        def _():
            for a in range(NT):
                prompt_copy(1, a, h).wait_send()

    for a in range(1, NT):
        resp_copy(a).wait_send()
    for piece in range(NPC, -1, -1):
        for a in range(1, NT):
            gather(piece, a).wait()
        for c in range(piece * PC, ROWS if piece == NPC else (piece + 1) * PC, 256):
            dk[c : c + 256, :] = ga[:DH, c : c + 256].T
            dv[c : c + 256, :] = ga[DH:, c : c + 256].T


def per_device(queries, keys, values, dout, offsets, lengths):
    V = pl.BlockSpec(memory_space=pltpu.VMEM)
    H = pl.BlockSpec(memory_space=pl.ANY)
    SM = pl.BlockSpec(memory_space=pltpu.SMEM)
    D = pltpu.SemaphoreType.DMA
    big = pltpu.VMEM((KEYS // 128, BQ, 128), f32)
    acc = pltpu.VMEM((KEYS // 128, DH, 128), f32)
    stat = pltpu.VMEM((BQ, 128), f32)
    return tuple(
        pl.pallas_call(
            kernel,
            out_shape=[jax.ShapeDtypeStruct((ROWS, DH), bf)] * 3,
            in_specs=[SM, SM, H, H, H, H],
            out_specs=[V, V, V],
            scratch_shapes=[
                pltpu.VMEM((KEYS, DH), bf), pltpu.VMEM((KEYS, DH), bf),
                acc, acc, big, big, big, big,
                stat, stat, stat, stat, stat, stat,
                pltpu.VMEM((BQ, DH), f32), pltpu.VMEM((ROWS + XR, DH), bf),
                pltpu.VMEM((DH, BQ), bf), pltpu.VMEM((DH, BQ), bf),
                pltpu.VMEM((8, KEYS), f32),
                pltpu.VMEM((ROWS + XR, DH), bf), pltpu.VMEM((XR, DH), bf),
                pltpu.VMEM((2 * DH, KEYS), bf), pltpu.VMEM((2 * NT, FT, PH), bf),
                pltpu.VMEM((NT, FT, R), bf), pltpu.VMEM((2 * DH, ROWS), bf),
                D((4,)), D((4,)), D((NPC, 2 * NT)), D((NPC, 2 * NT)), D((NT,)), D((NT,)),
                D((NPC + 1, NT)), D((NPC + 1, NT)), D((3,)), D((3,)), D((6,)),
            ],
            compiler_params=pltpu.CompilerParams(
                collective_id=0, has_side_effects=True, vmem_limit_bytes=60 * 2**20
            ),
        )(offsets, lengths, queries, keys, values, dout)
    )


def solution(mesh):
    return jax.shard_map(
        per_device,
        mesh=mesh,
        in_specs=(P("dp", "tensor"), P("dp", None), P("dp", None), P("dp", "tensor"), P(), P("dp")),
        out_specs=(P("dp", "tensor"), P("dp", None), P("dp", None)),
        check_vma=False,
    )
```

```python
import functools

import jax
import jax.numpy as jnp
from jax import lax
from jax.experimental import pallas as pl
from jax.experimental.pallas import tpu as pltpu
from jax.sharding import PartitionSpec as P

MESH = pl.DeviceIdType.MESH
f32 = jnp.float32
bf = jnp.bfloat16

PH = 2048
R = 1024
DH = 128
KEYS = 2 * PH + R
BQ, BK = 256, 512
RG = 32
T = BK // 128
NT = 8
FT = 2 * DH // NT
NPC = 4
PC = PH // NPC
HP = PH // 2
XR = 768
ROWS = PH + R
NEG = -1e30
EARLY = ()
SCALE = 1.0 / DH**0.5
CC = SCALE * 1.4426950408889634


def dot_nt(a, b):
    return lax.dot_general(a, b, (((1,), (1,)), ((), ())), preferred_element_type=f32)


def dot_nn(a, b):
    return jnp.dot(a, b, preferred_element_type=f32)


def kernel(
    offs, lens, q, kin, vin, do, dq, dk, dv,
    k, v, dkT, dvT, S, E, DP0, DP1, mx, mb, la, ta, rl, dl, dqa, dom, qT, dT, bias,
    qa, dqx, sb, rb, rr, ga,
    kv_s, kv_r, p_s, p_r, r_s, r_r, g_s, g_r, x_s, x_r, l_s,
):
    d = lax.axis_index("dp")
    t = lax.axis_index("tensor")
    half = lax.axis_size("dp") // 2
    side = lax.div(d, half)
    pair = lax.rem(d, half)
    offset = offs[pair]
    length = lens[0]

    def peer(b, a):
        return (lax.rem(side + b, 2) * half + pair, lax.rem(t + a, NT))

    own = pl.ds(pl.multiple_of(side * PH, PH), PH)
    loads = [
        pltpu.make_async_copy(src, dst, l_s.at[i])
        for i, (src, dst) in enumerate((
            (kin.at[pl.ds(0, PH)], k.at[own]), (kin.at[pl.ds(PH, R)], k.at[pl.ds(2 * PH, R)]),
            (vin.at[pl.ds(0, PH)], v.at[own]), (vin.at[pl.ds(PH, R)], v.at[pl.ds(2 * PH, R)]),
            (q, qa.at[pl.ds(0, ROWS)]), (do, dom.at[pl.ds(0, ROWS)]),
        ))
    ]
    for c in loads:
        c.start()

    barrier = pltpu.get_barrier_semaphore()
    for i in range(1, 2 * NT):
        pl.semaphore_signal(barrier, inc=1, device_id=peer(i // NT, i % NT), device_id_type=MESH)
    pl.semaphore_wait(barrier, 2 * NT - 1)

    flip = t + 1 - 2 * lax.rem(t, 2)
    kv = []
    for h in range(2):
        dst = (lax.rem(side + 1, 2) * half + pair, t if h == 0 else flip)
        for i, (src, to) in enumerate(((kin, k), (vin, v))):
            rows = pl.ds(pl.multiple_of(side * PH + h * HP, HP), HP)
            c = pltpu.make_async_remote_copy(
                src_ref=src.at[pl.ds(h * HP, HP)], dst_ref=to.at[rows],
                send_sem=kv_s.at[2 * h + i], recv_sem=kv_r.at[2 * h + i],
                device_id=dst, device_id_type=MESH,
            )
            c.start()
            kv.append(c)

    over = [
        pltpu.make_async_remote_copy(
            src_ref=src.at[pl.ds(PH - XR, XR)], dst_ref=to.at[pl.ds(ROWS, XR)],
            send_sem=x_s.at[i], recv_sem=x_r.at[i], device_id=peer(1, 0), device_id_type=MESH,
        )
        for i, (src, to) in enumerate(((q, qa), (do, dom)))
    ]
    back = pltpu.make_async_remote_copy(
        src_ref=dqx, dst_ref=dq.at[pl.ds(PH - XR, XR)],
        send_sem=x_s.at[2], recv_sem=x_r.at[2], device_id=peer(1, 0), device_id_type=MESH,
    )

    kp = lax.broadcasted_iota(jnp.int32, (8, KEYS), 1)
    bias[...] = jnp.where(kp >= offset, 0.0, NEG).astype(f32)
    dkT[...] = jnp.zeros_like(dkT)
    dvT[...] = jnp.zeros_like(dvT)
    for c in loads:
        c.wait()
    row = lax.broadcasted_iota(jnp.int32, (R, DH), 0)
    dom[PH:ROWS, :] = jnp.where(row < length, dom[PH:ROWS, :], jnp.zeros((R, DH), bf))

    NR, NP = R // BQ, PH // BQ
    NX = XR // BQ
    NB = NR + NP + NX - 2 * NX * side
    DPS = (DP0, DP1)

    def info(j):
        resp = j < NR
        extra = (side == 0) & (j >= NR) & (j < NR + NX)
        b = NB - 1 - j
        x = NR + NX - 1 - j
        row0 = jnp.where(resp, PH + (NR - 1 - j) * BQ, jnp.where(extra, ROWS + x * BQ, b * BQ))
        pos0 = jnp.where(resp, PH + row0, jnp.where(extra, 2 * PH - XR + x * BQ, side * PH + row0))
        n = jnp.where(j < NB, lax.div(pos0 + BQ - 1, BK) + 1, 0)
        return pl.multiple_of(jnp.maximum(row0, 0), BQ), pos0, n

    def ks(c):
        return pl.ds(pl.multiple_of(c * BK, BK), BK)

    def scores(slot, row0, pos0, c, masked, padded=True):
        DP = DPS[slot]
        s = dot_nt(qa[pl.ds(row0, BQ), :], k[ks(c), :])
        dp = dot_nt(dom[pl.ds(row0, BQ), :], v[ks(c), :])
        if masked:
            cols = lax.broadcasted_iota(jnp.int32, (RG, 128), 1)
        for r in range(0, BQ, RG):
            m = mx[r : r + RG, :]
            for i in range(T):
                st = s[r : r + RG, i * 128 : (i + 1) * 128]
                if masked:
                    rows = lax.broadcasted_iota(jnp.int32, (RG, 128), 0) + (pos0 - c * BK + r)
                    ct = cols + i * 128
                    ok = (ct < rows) & (ct + c * BK >= offset) | (ct == rows)
                    st = jnp.where(ok, st, NEG)
                elif padded:
                    st = st + bias[0:1, pl.ds(pl.multiple_of(c * BK + i * 128, 128), 128)]
                S[c * T + i, r : r + RG, :] = st
                m = jnp.maximum(m, st)
                DP[c * T + i, r : r + RG, :] = dp[r : r + RG, i * 128 : (i + 1) * 128]
            mx[r : r + RG, :] = m

    def expo(slot, c):
        DP = DPS[slot]
        for r in range(0, BQ, RG):
            l, tt, m = la[r : r + RG, :], ta[r : r + RG, :], mb[r : r + RG, :]
            for i in range(T):
                e = jnp.exp2(S[c * T + i, r : r + RG, :] * CC - m)
                l = l + e
                tt = tt + e * DP[c * T + i, r : r + RG, :]
                E[c * T + i, r : r + RG, :] = e
            la[r : r + RG, :] = l
            ta[r : r + RG, :] = tt

    def grads_in(slot, c):
        DP = DPS[slot]
        ps, xs = [], []
        for r in range(0, BQ, RG):
            rv, dd = rl[r : r + RG, :], dl[r : r + RG, :]
            pr, xr = [], []
            for i in range(T):
                p = E[c * T + i, r : r + RG, :] * rv
                x = p * (DP[c * T + i, r : r + RG, :] - dd)
                pr.append(p.astype(bf))
                xr.append(x.astype(bf))
            ps.append(jnp.concatenate(pr, 1))
            xs.append(jnp.concatenate(xr, 1))
        return jnp.concatenate(ps, 0), jnp.concatenate(xs, 0)

    def grads_out(c, p, x):
        gv = dot_nn(dT[...], p)
        gk = dot_nn(qT[...], x)
        for i in range(T):
            dvT[c * T + i] += gv[:, i * 128 : (i + 1) * 128]
            dkT[c * T + i] += gk[:, i * 128 : (i + 1) * 128]
        dqa[...] += dot_nn(x, k[ks(c), :])

    def row_max():
        mb[...] = jnp.broadcast_to(jnp.max(mx[...], axis=1, keepdims=True) * CC, (BQ, 128))
        mx[...] = jnp.full((BQ, 128), NEG, f32)

    def row_sums():
        inv = 1.0 / jnp.sum(la[...], axis=1, keepdims=True)
        rl[...] = jnp.broadcast_to(inv, (BQ, 128))
        dl[...] = jnp.broadcast_to(jnp.sum(ta[...], axis=1, keepdims=True) * inv, (BQ, 128))
        la[...] = jnp.zeros((BQ, 128), f32)
        ta[...] = jnp.zeros((BQ, 128), f32)

    def turn(row):
        qT[...] = qa[pl.ds(row, BQ), :].T
        dT[...] = dom[pl.ds(row, BQ), :].T
        dqa[...] = jnp.zeros((BQ, DH), f32)

    def loop(lo, hi, f):
        def body(c, _):
            f(c)
            return 0

        lax.fori_loop(lo, hi, body, 0)

    def feats(a):
        return pl.ds(pl.multiple_of(lax.rem(t + a, NT) * FT, FT), FT)

    def prompt_copy(b, a, h):
        cols = pl.ds(pl.multiple_of(lax.rem(side + b, 2) * PH + h * PC, PC), PC)
        i = b * NT + a
        return pltpu.make_async_remote_copy(
            src_ref=sb.at[feats(a), cols], dst_ref=rb.at[i, :, pl.ds(h * PC, PC)],
            send_sem=p_s.at[h, i], recv_sem=p_r.at[h, i],
            device_id=peer(b, a), device_id_type=MESH,
        )

    def resp_copy(a):
        return pltpu.make_async_remote_copy(
            src_ref=sb.at[feats(a), pl.ds(2 * PH, R)], dst_ref=rr.at[a],
            send_sem=r_s.at[a], recv_sem=r_r.at[a],
            device_id=peer(0, a), device_id_type=MESH,
        )

    def gather(piece, a):
        cols = pl.ds(piece * PC, PC if piece < NPC else R)
        return pltpu.make_async_remote_copy(
            src_ref=ga.at[feats(0), cols], dst_ref=ga.at[feats(0), cols],
            send_sem=g_s.at[piece, a], recv_sem=g_r.at[piece, a],
            device_id=peer(0, a), device_id_type=MESH,
        )

    def pack(c0, tiles):
        def one(i):
            c = c0 + i
            cols = pl.ds(pl.multiple_of(c * 128, 128), 128)
            sb[:DH, cols] = (dkT[c] * SCALE).astype(bf)
            sb[DH:, cols] = dvT[c].astype(bf)

        loop(0, tiles, one)

    HT = PC // 128

    def send_resp():
        pack(2 * PH // 128, R // 128)
        for a in range(1, NT):
            resp_copy(a).start()

    def send_prompt(b, h):
        pack(lax.rem(side + b, 2) * NPC * HT + h * HT, HT)
        for a in range(0 if b else 1, NT):
            prompt_copy(b, a, h).start()

    def finish_resp():
        for a in range(1, NT):
            resp_copy(a).wait_recv()

        def tile(c):
            cols = pl.ds(pl.multiple_of(c * 128, 128), 128)
            total = sb[feats(0), pl.ds(pl.multiple_of(2 * PH + c * 128, 128), 128)].astype(f32)
            for a in range(1, NT):
                total = total + rr[a, :, cols].astype(f32)
            ga[feats(0), pl.ds(pl.multiple_of(PH + c * 128, 128), 128)] = total.astype(bf)

        loop(0, R // 128, tile)
        for a in range(1, NT):
            gather(NPC, a).start()

    def finish_prompt(h):
        for i in range(1, 2 * NT):
            prompt_copy(i // NT, i % NT, h).wait_recv()

        def tile(c):
            cols = pl.ds(pl.multiple_of(h * PC + c * 128, 128), 128)
            mine = pl.ds(pl.multiple_of(side * PH + h * PC + c * 128, 128), 128)
            total = sb[feats(0), mine].astype(f32)
            for i in range(1, 2 * NT):
                total = total + rb[i, :, cols].astype(f32)
            ga[feats(0), cols] = total.astype(bf)

        loop(0, HT, tile)
        for a in range(1, NT):
            gather(h, a).start()

    mx[...] = jnp.full((BQ, 128), NEG, f32)
    la[...] = jnp.zeros((BQ, 128), f32)
    ta[...] = jnp.zeros((BQ, 128), f32)
    row_a, pos_a, na = info(jnp.int32(0))
    row_b, pos_b, nb = info(jnp.int32(1))
    PB = PH // BK
    loop(side * PB, side * PB + PB, lambda c: scores(0, row_a, pos_a, c, False))
    loop(2 * PB, na - 1, lambda c: scores(0, row_a, pos_a, c, False))
    scores(0, row_a, pos_a, na - 1, True)
    for c in kv:
        c.wait_recv()

    @pl.when(side == 1)
    def _():
        for c in kv:
            c.wait_send()
        for c in over:
            c.start()

    loop(PB - side * PB, 2 * PB - side * PB, lambda c: scores(0, row_a, pos_a, c, False))
    row_max()

    def first(c, masked=False):
        expo(0, c)
        scores(1, row_b, pos_b, c, masked)

    loop(0, nb - 1, first)
    first(nb - 1, True)
    loop(nb, na, lambda c: expo(0, c))
    row_sums()
    row_max()
    turn(row_a)

    def block(j, slot):
        r0, _, n0 = info(j)
        r1, _, n1 = info(j + 1)
        r2, p2, n2 = info(j + 2)

        def three(c, masked=False, padded=True):
            p, x = grads_in(slot, c)
            expo(1 - slot, c)
            scores(slot, r2, p2, c, masked, padded)
            grads_out(c, p, x)

        def two_of(c):
            p, x = grads_in(slot, c)
            expo(1 - slot, c)
            grads_out(c, p, x)

        def one_of(c):
            grads_out(c, *grads_in(slot, c))

        loop(0, jnp.minimum(n2 - 1, PH // BK), three)
        loop(PH // BK, n2 - 1, lambda c: three(c, padded=False))

        @pl.when(n2 > 0)
        def _():
            three(n2 - 1, True)

        loop(n2, n1, two_of)
        loop(n1, n0, one_of)
        @pl.when((r0 < ROWS) & (n0 > 0))
        def _():
            dq[pl.ds(r0, BQ), :] = (dqa[...] * SCALE).astype(bf)

        @pl.when(r0 >= ROWS)
        def _():
            dqx[pl.ds(pl.multiple_of(r0 - ROWS, BQ), BQ), :] = (dqa[...] * SCALE).astype(bf)


        @pl.when(n1 > 0)
        def _():
            row_sums()
            row_max()
            turn(r1)

        @pl.when(j == NR - 1)
        def _():
            send_resp()

            @pl.when(side == 1)
            def _():
                for h in range(-((NX - NP) // 2), NPC):
                    send_prompt(0, h)

        @pl.when((side == 0) & (j == NR + NX - 1))
        def _():
            back.start()
            for h in range(NPC - 1, -1, -1):
                send_prompt(1, h)

        @pl.when(j == NR + 1)
        def _():
            finish_resp()

        b = NB - 1 - j
        for h in range(1, NPC):

            @pl.when((b == 2 * h) & (j >= NR + NX - NX * side))
            def _():
                send_prompt(0, h)

        @pl.when((side == 0) & (b == 1))
        def _():
            for h in EARLY:
                finish_prompt(h)

    def two(i):
        @pl.when((side == 0) & (i == 1))
        def _():
            for c in over:
                c.wait_recv()

        block(2 * i, 0)
        block(2 * i + 1, 1)

    loop(0, lax.div(NB + 1, 2), two)

    @pl.when(side == 1)
    def _():
        for h in range(NPC - 1, -1, -1):
            send_prompt(1, h)

    send_prompt(0, 0)

    @pl.when(side == 1)
    def _():
        for h in range(NPC):
            for a in range(NT):
                prompt_copy(1, a, h).wait_send()
        for h in EARLY:
            finish_prompt(h)

    for h in range(NPC - 1, -1, -1):
        if h not in EARLY:
            finish_prompt(h)

    @pl.when(side == 0)
    def _():
        back.wait_send()
        for c in kv:
            c.wait_send()

    @pl.when(side == 1)
    def _():
        back.wait_recv()
        for c in over:
            c.wait_send()

    for h in range(NPC):
        for a in range(1, NT):
            prompt_copy(0, a, h).wait_send()

        @pl.when(side == 0)
        def _():
            for a in range(NT):
                prompt_copy(1, a, h).wait_send()

    for a in range(1, NT):
        resp_copy(a).wait_send()
    for piece in range(NPC, -1, -1):
        for a in range(1, NT):
            gather(piece, a).wait()
        for c in range(piece * PC, ROWS if piece == NPC else (piece + 1) * PC, 256):
            dk[c : c + 256, :] = ga[:DH, c : c + 256].T
            dv[c : c + 256, :] = ga[DH:, c : c + 256].T


def per_device(queries, keys, values, dout, offsets, lengths):
    V = pl.BlockSpec(memory_space=pltpu.VMEM)
    H = pl.BlockSpec(memory_space=pl.ANY)
    SM = pl.BlockSpec(memory_space=pltpu.SMEM)
    D = pltpu.SemaphoreType.DMA
    big = pltpu.VMEM((KEYS // 128, BQ, 128), f32)
    acc = pltpu.VMEM((KEYS // 128, DH, 128), f32)
    stat = pltpu.VMEM((BQ, 128), f32)
    return tuple(
        pl.pallas_call(
            kernel,
            out_shape=[jax.ShapeDtypeStruct((ROWS, DH), bf)] * 3,
            in_specs=[SM, SM, H, H, H, H],
            out_specs=[V, V, V],
            scratch_shapes=[
                pltpu.VMEM((KEYS, DH), bf), pltpu.VMEM((KEYS, DH), bf),
                acc, acc, big, big, big, big,
                stat, stat, stat, stat, stat, stat,
                pltpu.VMEM((BQ, DH), f32), pltpu.VMEM((ROWS + XR, DH), bf),
                pltpu.VMEM((DH, BQ), bf), pltpu.VMEM((DH, BQ), bf),
                pltpu.VMEM((8, KEYS), f32),
                pltpu.VMEM((ROWS + XR, DH), bf), pltpu.VMEM((XR, DH), bf),
                pltpu.VMEM((2 * DH, KEYS), bf), pltpu.VMEM((2 * NT, FT, PH), bf),
                pltpu.VMEM((NT, FT, R), bf), pltpu.VMEM((2 * DH, ROWS), bf),
                D((4,)), D((4,)), D((NPC, 2 * NT)), D((NPC, 2 * NT)), D((NT,)), D((NT,)),
                D((NPC + 1, NT)), D((NPC + 1, NT)), D((3,)), D((3,)), D((6,)),
            ],
            compiler_params=pltpu.CompilerParams(
                collective_id=0, has_side_effects=True, vmem_limit_bytes=60 * 2**20
            ),
        )(offsets, lengths, queries, keys, values, dout)
    )


def solution(mesh):
    return jax.shard_map(
        per_device,
        mesh=mesh,
        in_specs=(P("dp", "tensor"), P("dp", None), P("dp", None), P("dp", "tensor"), P(), P("dp")),
        out_specs=(P("dp", "tensor"), P("dp", None), P("dp", None)),
        check_vma=False,
    )
```
